256 devices in a mesh: dp: 32 (over y_lo, z, core), mp: 8 (over y_hi, x).
Axes of the slice: x: 4, y: 4 (y_hi: 2, y_lo: 2; y = y_hi * 2 + y_lo), z: 8, core: 2. Of those that a mesh axis runs over, the one named last changes fastest.
Arguments:
- tokens: bfloat16 [2048, 5120], P('dp', 'mp'), may hold values from -6 to 6, as said below
- gate_first: bfloat16 [13824, 5120], P('dp', 'mp'), may hold values from -6 to 6
- up_first: bfloat16 [13824, 5120], P('dp', 'mp'), may hold values from -6 to 6
- down_first: bfloat16 [13824, 5120], P('dp', 'mp'), may hold values from -6 to 6
- gate_second: bfloat16 [13824, 5120], P('dp', 'mp'), may hold values from -6 to 6
- up_second: bfloat16 [13824, 5120], P('dp', 'mp'), may hold values from -6 to 6
- down_second: bfloat16 [13824, 5120], P('dp', 'mp'), may hold values from -6 to 6
- matching: int32 [13824], replicated, may hold values from 0 to 13823, as said below
Outputs:
- merged_gate: bfloat16 [13824, 5120], P('dp', 'mp')
- merged_up: bfloat16 [13824, 5120], P('dp', 'mp')
- merged_down: bfloat16 [13824, 5120], P('dp', 'mp')
- correlation: float32 [6912, 13824], P('mp', 'dp')
The draws below stay inside these ranges and needn't reach their ends.
Inputs may be any that keep to these rules, and one draw needn't show every extreme that they name: matching is a permutation; for any aligned block of 432 positions and any aligned block of 432 values, at most 14 of the block's entries lie in that block of values, and in every draw some pair of blocks holds exactly 14. `tokens`: each token's 5120 features have a mean square within a few hundredths of 1.
All inputs are finite; a program needn't handle non-finite values.
Results may differ from the reference program's by a relative error of at most 0.028.
Values may be sent and summed in bfloat16 or wider, within the bound.
No kernel may reach another device: no remote copies, remote signals or barrier semaphores. Data moves between devices by JAX's collectives and lax.ppermute only.
A program may use at most 64 MiB of HBM per device.

```python
import math
import jax
import jax.numpy as jnp
from jax import lax

D = 5120
FF = 13824
CROWS = 216
TOKENS = 2048
N_DP = 32
N_MP = 8


def draw_matching(key, part):
    unit_count = FF // N_DP
    key_dest = jax.random.fold_in(key, 11)
    key_blocks = jax.random.fold_in(key, 12)
    key_source = jax.random.fold_in(key, 13)
    dest_shuffle = jax.vmap(lambda sub: jax.random.permutation(sub, unit_count))(jax.random.split(key_dest, N_DP))
    block_order = jax.random.permutation(key_blocks, N_DP)
    source_shuffle = jax.vmap(lambda sub: jax.random.permutation(sub, unit_count))(jax.random.split(key_source, N_DP))
    dest_ids = jnp.arange(N_DP, dtype=jnp.int32)[:, None]
    ranked = dest_shuffle.astype(jnp.int32) * N_DP + dest_ids
    source_block = ranked // unit_count
    source_offset = ranked % unit_count
    blocks = block_order.astype(jnp.int32)[source_block]
    offsets = source_shuffle.astype(jnp.int32)[blocks, source_offset]
    return (blocks * unit_count + offsets).reshape(-1).astype(jnp.int32)


def draw_tokens(key, part):
    key_rough = jax.random.fold_in(key, 21)
    raw = jax.random.normal(key_rough, (TOKENS, D), jnp.float32)
    raw = jnp.clip(raw, -5.0, 5.0)
    spread = jnp.sqrt(jnp.mean(raw * raw, axis=1, keepdims=True))
    return (raw / spread).astype(jnp.bfloat16)


def steps_of(rng, shape, cuts, low, top_value):
    factor_of, own = 1.0, jax.random.fold_in(rng, 6)
    for axis_at, parts in cuts:
        steps = jnp.exp(jax.random.uniform(jax.random.fold_in(own, axis_at), (parts,), jnp.float32, low / len(cuts), top_value / len(cuts)))
        factor_of = factor_of * jnp.repeat(steps, shape[axis_at] // parts).reshape([-1 if axis == axis_at else 1 for axis in range(len(shape))])
    return factor_of


def normal_values(rng, extent, scale, bound, shards=(), kind=jnp.bfloat16):
    drawn = jax.random.normal(rng, extent, jnp.float32) * scale
    if len(shards) > 0:
        drawn = steps_of(rng, extent, shards, -0.22, 0.18) * drawn
    return jnp.clip(drawn, min=-bound, max=bound).astype(kind)


def setup_inputs(seed: int = 0) -> dict:
    splits = jax.random.split(jax.random.key(seed), 9)
    return {
        "tokens": draw_tokens(jax.random.fold_in(splits[8], 71), 0),
        "gate_first": normal_values(splits[1], (FF, D), 1.0, 6.0, ((0, 32), (1, 8))),
        "up_first": normal_values(splits[2], (FF, D), 1.0, 6.0, ((0, 32), (1, 8))),
        "down_first": normal_values(splits[3], (FF, D), 1.0, 6.0, ((0, 32), (1, 8))),
        "gate_second": normal_values(splits[4], (FF, D), 1.0, 6.0, ((0, 32), (1, 8))),
        "up_second": normal_values(splits[5], (FF, D), 1.0, 6.0, ((0, 32), (1, 8))),
        "down_second": normal_values(splits[6], (FF, D), 1.0, 6.0, ((0, 32), (1, 8))),
        "matching": draw_matching(jax.random.fold_in(splits[8], 71), 0),
    }


def projected(inputs, weight):
    feature_cols = D // N_MP
    factor = 1.0 / math.sqrt(D)
    summed = jnp.zeros((TOKENS, FF), jnp.float32)
    for piece in range(N_MP):
        inner = inputs[:, piece * feature_cols:(piece + 1) * feature_cols]
        outer = weight[:, piece * feature_cols:(piece + 1) * feature_cols]
        term = lax.dot_general(inner, outer, (((1,), (1,)), ((), ())), preferred_element_type=jnp.float32)
        term = (term * factor).astype(jnp.bfloat16)
        term = lax.optimization_barrier(term)
        summed = summed + term.astype(jnp.float32)
    return summed

def averaged(first, second, matching):
    moved = jnp.take(second, matching, axis=0)
    return ((first.astype(jnp.float32) + moved.astype(jnp.float32)) * 0.5).astype(jnp.bfloat16)

def reference(tokens, gate_first, up_first, down_first, gate_second, up_second, down_second, matching):
    hidden_first = (jax.nn.silu(projected(tokens, gate_first)) * projected(tokens, up_first)).astype(jnp.bfloat16)
    hidden_second = (jax.nn.silu(projected(tokens, gate_second)) * projected(tokens, up_second)).astype(jnp.bfloat16)
    window = hidden_first.reshape(TOKENS, N_DP, FF // N_DP)[:, :, :CROWS].reshape(TOKENS, CROWS * N_DP)
    chosen = jnp.take(hidden_second, matching, axis=1)
    correlation = lax.dot_general(window, chosen, (((0,), (0,)), ((), ())), preferred_element_type=jnp.float32)
    correlation = correlation / math.sqrt(TOKENS)
    return (averaged(gate_first, gate_second, matching), averaged(up_first, up_second, matching), averaged(down_first, down_second, matching), correlation)
```

```python
import math

import jax
import jax.numpy as jnp
from jax import lax
from jax.sharding import Mesh
from jax.sharding import PartitionSpec as P

D = 5120
CROWS = 216
CAPACITY = 14
AXES = ("y_lo", "z", "core", "y_hi", "x")
DP = ("y_lo", "z", "core")
MP = ("y_hi", "x")
CHIPS = ("y_lo", "z")
BF = jnp.bfloat16
F32 = jnp.float32


def shifted(x, axis, k):
    n = lax.axis_size(axis)
    return lax.ppermute(x, axis, [(i, (i + k) % n) for i in range(n)])


def swapped(x, axis):
    return lax.ppermute(x, axis, [(0, 1), (1, 0)])


def ring(block, axis):
    n = lax.axis_size(axis)
    up = down = block
    found = [(0, block)]
    for k in range(1, n // 2):
        up = shifted(up, axis, 1)
        down = shifted(down, axis, -1)
        found += [(n - k, up), (k, down)]
    half = block.shape[0] // 2
    far = jnp.concatenate(
        [shifted(up[:half], axis, 1), shifted(down[half:], axis, -1)], axis=0
    )
    return [*found, (n // 2, far)]


def mp_perm(dy, dx):
    return [(y * 4 + x, (y ^ dy) * 4 + (x + dx) % 4) for y in range(2) for x in range(4)]


def window_perm():
    def flat(yl, z, c, yh, x):
        return (((yl * 8 + z) * 2 + c) * 2 + yh) * 4 + x

    return [
        (flat(yl, z, c, yh, x), flat(yh, x * 2 + z % 2, c, yl, z // 2))
        for yl in range(2)
        for z in range(8)
        for c in range(2)
        for yh in range(2)
        for x in range(4)
    ]


def one_hot(index, size):
    return (index[:, None] == lax.broadcasted_iota(jnp.int32, (index.shape[0], size), 1)).astype(BF)


def mm(a, b):
    return jnp.dot(a, b, preferred_element_type=F32)


def nt(a, b):
    return lax.dot_general(a, b, (((1,), (1,)), ((), ())), preferred_element_type=F32)


def routes(matching, count, me, capacity):
    groups = matching.reshape(-1, count)
    number = groups.shape[0]
    owned = lax.div(groups, count) == me
    before = lax.broadcasted_iota(jnp.int32, (count, count), 0) < lax.broadcasted_iota(
        jnp.int32, (count, count), 1
    )
    before = before.astype(BF)
    rank = mm(owned.astype(BF), before).astype(jnp.int32)
    slots = jnp.arange(capacity, dtype=jnp.int32)
    picked = owned[:, None, :] & (rank[:, None, :] == slots[None, :, None])
    offsets = lax.rem(groups, count)
    send = jnp.sum(jnp.where(picked, offsets[:, None, :], 0), axis=2).reshape(-1)
    mine = lax.dynamic_slice_in_dim(matching, me * count, count)
    owner = lax.div(mine, count)
    from_block = owner[:, None] == lax.broadcasted_iota(jnp.int32, (count, number), 1)
    arrival = lax.dot_general(
        before, from_block.astype(BF), (((0,), (0,)), ((), ())), preferred_element_type=F32
    )
    arrival = jnp.sum(jnp.where(from_block, arrival, 0.0), axis=1).astype(jnp.int32)
    return one_hot(send, count), owner * capacity + arrival


def activated(pre, count):
    return (jax.nn.silu(pre[:count]) * pre[count:]).astype(BF)


def local(tokens, gate_first, up_first, down_first, gate_second, up_second, down_second, matching):
    units, feats = gate_first.shape
    yl, z, c = (lax.axis_index(a) for a in DP)
    m = lax.axis_index(MP)
    chip = lax.axis_index(CHIPS)
    rows = tokens.shape[0] * 2
    factor = 1.0 / math.sqrt(D)

    def ordered(mine, other, index):
        first = index == 0
        return jnp.concatenate([jnp.where(first, mine, other), jnp.where(first, other, mine)], axis=0)

    with jax.named_scope("weights_of_chip"):
        first_mine = jnp.concatenate([gate_first[:CROWS], up_first[:CROWS]], axis=0)
        second_mine = jnp.concatenate([gate_second, up_second], axis=0)
        first_other = swapped(first_mine, "core")
        second_other = swapped(second_mine, "core")
        first_chip = jnp.concatenate(
            [
                ordered(first_mine[:CROWS], first_other[:CROWS], c),
                ordered(first_mine[CROWS:], first_other[CROWS:], c),
            ],
            axis=0,
        )
        second_chip = jnp.concatenate(
            [
                ordered(second_mine[:units], second_other[:units], c),
                ordered(second_mine[units:], second_other[units:], c),
            ],
            axis=0,
        )

    with jax.named_scope("tokens"):
        pair = ordered(tokens, swapped(tokens, "y_lo"), yl)
        held = jnp.zeros((8, rows, feats), BF)
        for k, block in ring(pair, "z"):
            held = lax.dynamic_update_slice(held, block[None], (lax.rem(z + k, 8), 0, 0))

    with jax.named_scope("routing"):
        row_send, row_land = routes(matching, units, lax.axis_index(DP), CAPACITY)
        act_send, act_land = routes(matching, 2 * units, chip, 4 * CAPACITY)
        row_place = one_hot(row_land, 32 * CAPACITY)
        act_land = jnp.where(c == 0, act_land, jnp.roll(act_land, units))
        act_place = one_hot(act_land, 16 * 4 * CAPACITY)

    def exchanged(weights):
        total = None
        for dy, dx in ((1, 2), (0, 2), (1, 1), (1, 3), (0, 1), (0, 3), (1, 0), (0, 0)):
            to = (lax.div(m, 4) ^ dy) * 4 + lax.rem(m + dx, 4)
            block = lax.dynamic_index_in_dim(held, to, 0, keepdims=False)
            term = (nt(weights, block) * factor).astype(BF)
            if (dy, dx) != (0, 0):
                term = lax.ppermute(term, MP, mp_perm(dy, dx))
            total = term.astype(F32) if total is None else total + term.astype(F32)
        return total

    with jax.named_scope("second_sums"):
        hidden_second = activated(exchanged(second_chip), 2 * units)
    with jax.named_scope("first_sums"):
        hidden_first = activated(exchanged(first_chip), 2 * CROWS)

    with jax.named_scope("matched"):
        outgoing = mm(act_send, hidden_second).astype(BF).reshape(16, 4 * CAPACITY, rows)
        incoming = lax.all_to_all(outgoing, CHIPS, split_axis=0, concat_axis=0, tiled=True)
        chosen = mm(act_place, incoming.reshape(-1, rows)).astype(BF)
        both = jnp.stack([chosen, swapped(chosen, "y_hi")])
        y_hi, x = lax.axis_index("y_hi"), lax.axis_index("x")
        full_chosen = jnp.zeros((2 * units, 8 * rows), BF)
        for k, block in ring(both, "x"):
            for j in range(2):
                at = (y_hi ^ j) * 4 + lax.rem(x + k, 4)
                full_chosen = lax.dynamic_update_slice(full_chosen, block[j], (0, at * rows))

    with jax.named_scope("window"):
        window = lax.ppermute(hidden_first, AXES, window_perm())
        both = jnp.stack([window, swapped(window, "y_lo")])
        full_window = jnp.zeros((2, 2 * CROWS, 8 * rows), BF)
        for k, block in ring(both, "z"):
            at_z = lax.rem(z + k, 8)
            for j in range(2):
                at = (yl ^ j) * 4 + lax.div(at_z, 2)
                full_window = lax.dynamic_update_slice(
                    full_window, block[j][None], (lax.rem(at_z, 2), 0, at * rows)
                )
        full_window = full_window.reshape(4 * CROWS, 8 * rows)

    with jax.named_scope("rows"):
        second_rows = jnp.concatenate([gate_second, up_second, down_second], axis=1)
        outgoing_rows = mm(row_send, second_rows).astype(BF).reshape(32, CAPACITY, 3 * feats)
        incoming_rows = lax.all_to_all(outgoing_rows, DP, split_axis=0, concat_axis=0, tiled=True)
        moved = mm(row_place, incoming_rows.reshape(-1, 3 * feats))

        def averaged(first, second):
            return ((first.astype(F32) + second) * 0.5).astype(BF)

        merged = (
            averaged(gate_first, moved[:, :feats]),
            averaged(up_first, moved[:, feats : 2 * feats]),
            averaged(down_first, moved[:, 2 * feats :]),
        )

    with jax.named_scope("correlation"):
        theirs = swapped(nt(full_window, full_chosen[units:]), "core")
        correlation = (nt(full_window, full_chosen[:units]) + theirs) * (1.0 / math.sqrt(16 * rows))
    return (*merged, correlation)


def solution(mesh):
    split = Mesh(mesh.devices.reshape(2, 8, 2, 2, 4), AXES)
    placed = (*(P(DP, MP),) * 7, P())
    return jax.shard_map(
        local,
        mesh=split,
        in_specs=placed,
        out_specs=(P(DP, MP), P(DP, MP), P(DP, MP), P(MP, DP)),
        check_vma=False,
    )
```

```python
import math

import jax
import jax.numpy as jnp
from jax import lax
from jax.sharding import Mesh
from jax.sharding import PartitionSpec as P

D = 5120
CROWS = 216
CAPACITY = 14
ROUTES = ((1, 2), (0, 2), (1, 1), (1, 3), (0, 1), (0, 3), (1, 0), (0, 0))
AXES = ("y_lo", "z", "core", "y_hi", "x")
DP = ("y_lo", "z", "core")
MP = ("y_hi", "x")
CHIPS = ("y_lo", "z")
BF = jnp.bfloat16
F32 = jnp.float32


def shifted(x, axis, k):
    n = lax.axis_size(axis)
    return lax.ppermute(x, axis, [(i, (i + k) % n) for i in range(n)])


def swapped(x, axis):
    return lax.ppermute(x, axis, [(0, 1), (1, 0)])


def ring(block, axis):
    n = lax.axis_size(axis)
    up = down = block
    found = [(0, block)]
    for k in range(1, n // 2):
        up = shifted(up, axis, 1)
        down = shifted(down, axis, -1)
        found += [(n - k, up), (k, down)]
    half = block.shape[0] // 2
    far = jnp.concatenate(
        [shifted(up[:half], axis, 1), shifted(down[half:], axis, -1)], axis=0
    )
    return [*found, (n // 2, far)]


def mp_perm(dy, dx):
    return [(y * 4 + x, (y ^ dy) * 4 + (x + dx) % 4) for y in range(2) for x in range(4)]


def window_perm():
    def flat(yl, z, c, yh, x):
        return (((yl * 8 + z) * 2 + c) * 2 + yh) * 4 + x

    return [
        (flat(yl, z, c, yh, x), flat(yh, x * 2 + z % 2, c, yl, z // 2))
        for yl in range(2)
        for z in range(8)
        for c in range(2)
        for yh in range(2)
        for x in range(4)
    ]


def one_hot(index, size):
    return (index[:, None] == lax.broadcasted_iota(jnp.int32, (index.shape[0], size), 1)).astype(BF)


def mm(a, b):
    return jnp.dot(a, b, preferred_element_type=F32)


def nt(a, b):
    return lax.dot_general(a, b, (((1,), (1,)), ((), ())), preferred_element_type=F32)


def routes(matching, count, me, capacity):
    groups = matching.reshape(-1, count)
    number = groups.shape[0]
    owned = lax.div(groups, count) == me
    before = lax.broadcasted_iota(jnp.int32, (count, count), 0) < lax.broadcasted_iota(
        jnp.int32, (count, count), 1
    )
    before = before.astype(BF)
    rank = mm(owned.astype(BF), before).astype(jnp.int32)
    slots = jnp.arange(capacity, dtype=jnp.int32)
    picked = owned[:, None, :] & (rank[:, None, :] == slots[None, :, None])
    offsets = lax.rem(groups, count)
    send = jnp.sum(jnp.where(picked, offsets[:, None, :], 0), axis=2).reshape(-1)
    mine = lax.dynamic_slice_in_dim(matching, me * count, count)
    owner = lax.div(mine, count)
    from_block = owner[:, None] == lax.broadcasted_iota(jnp.int32, (count, number), 1)
    arrival = lax.dot_general(
        before, from_block.astype(BF), (((0,), (0,)), ((), ())), preferred_element_type=F32
    )
    arrival = jnp.sum(jnp.where(from_block, arrival, 0.0), axis=1).astype(jnp.int32)
    return one_hot(send, count), owner * capacity + arrival


def activated(pre, count):
    return (jax.nn.silu(pre[:count]) * pre[count:]).astype(BF)


def local(tokens, gate_first, up_first, down_first, gate_second, up_second, down_second, matching):
    units, feats = gate_first.shape
    yl, z, c = (lax.axis_index(a) for a in DP)
    m = lax.axis_index(MP)
    chip = lax.axis_index(CHIPS)
    rows = tokens.shape[0] * 2
    factor = 1.0 / math.sqrt(D)

    def ordered(mine, other, index):
        first = index == 0
        return jnp.concatenate([jnp.where(first, mine, other), jnp.where(first, other, mine)], axis=0)

    with jax.named_scope("tokens"):
        pair = ordered(tokens, swapped(tokens, "y_lo"), yl)

    pair, gate_first, up_first, gate_second, up_second, down_second, matching = lax.optimization_barrier(
        (pair, gate_first, up_first, gate_second, up_second, down_second, matching)
    )

    with jax.named_scope("weights_of_chip"):
        first_mine = jnp.concatenate([gate_first[:CROWS], up_first[:CROWS]], axis=0)
        second_mine = jnp.concatenate([gate_second, up_second], axis=0)
        first_other = swapped(first_mine, "core")
        second_other = swapped(second_mine, "core")
        first_chip = jnp.concatenate(
            [
                ordered(first_mine[:CROWS], first_other[:CROWS], c),
                ordered(first_mine[CROWS:], first_other[CROWS:], c),
            ],
            axis=0,
        )
        second_chip = jnp.concatenate(
            [
                ordered(second_mine[:units], second_other[:units], c),
                ordered(second_mine[units:], second_other[units:], c),
            ],
            axis=0,
        )

    with jax.named_scope("tokens"):
        held = jnp.zeros((8, rows, feats), BF)
        for k, block in ring(pair, "z"):
            held = lax.dynamic_update_slice(held, block[None], (lax.rem(z + k, 8), 0, 0))

    with jax.named_scope("routing"):
        row_send, row_land = routes(matching, units, lax.axis_index(DP), CAPACITY)
        act_send, act_land = routes(matching, 2 * units, chip, 4 * CAPACITY)
        row_place = one_hot(row_land, 32 * CAPACITY)
        act_land = jnp.where(c == 0, act_land, jnp.roll(act_land, units))
        act_place = one_hot(act_land, 16 * 4 * CAPACITY)

    def terms(weights):
        found = []
        for dy, dx in ROUTES:
            to = (lax.div(m, 4) ^ dy) * 4 + lax.rem(m + dx, 4)
            block = lax.dynamic_index_in_dim(held, to, 0, keepdims=False)
            found.append((nt(weights, block) * factor).astype(BF))
        return found

    def exchanged(parts):
        total = parts[-1].astype(F32)
        for (dy, dx), part in zip(ROUTES[:-1], parts[:-1]):
            total = total + lax.ppermute(part, MP, mp_perm(dy, dx)).astype(F32)
        return total

    with jax.named_scope("rows"):
        row_send, held = lax.optimization_barrier((row_send, held))
        second_rows = jnp.concatenate([gate_second, up_second, down_second], axis=1)
        outgoing_rows = mm(row_send, second_rows).astype(BF).reshape(32, CAPACITY, 3 * feats)
        incoming_rows = lax.all_to_all(outgoing_rows, DP, split_axis=0, concat_axis=0, tiled=True)

    with jax.named_scope("second_sums"):
        hidden_second = activated(exchanged(terms(second_chip)), 2 * units)
        outgoing = mm(act_send, hidden_second).astype(BF).reshape(16, 4 * CAPACITY, rows)

    outgoing, first_chip, held, incoming_rows = lax.optimization_barrier(
        (outgoing, first_chip, held, incoming_rows)
    )

    with jax.named_scope("first_sums"):
        hidden_first = activated(exchanged(terms(first_chip)), 2 * CROWS)

    with jax.named_scope("matched"):
        incoming = lax.all_to_all(outgoing, CHIPS, split_axis=0, concat_axis=0, tiled=True)
        chosen = mm(act_place, incoming.reshape(-1, rows)).astype(BF)
        both = jnp.stack([chosen, swapped(chosen, "y_hi")])
        y_hi, x = lax.axis_index("y_hi"), lax.axis_index("x")
        full_chosen = jnp.zeros((2 * units, 8 * rows), BF)
        for k, block in ring(both, "x"):
            for j in range(2):
                at = (y_hi ^ j) * 4 + lax.rem(x + k, 4)
                full_chosen = lax.dynamic_update_slice(full_chosen, block[j], (0, at * rows))

    with jax.named_scope("window"):
        window = lax.ppermute(hidden_first, AXES, window_perm())
        both = jnp.stack([window, swapped(window, "y_lo")])
        full_window = jnp.zeros((2, 2 * CROWS, 8 * rows), BF)
        for k, block in ring(both, "z"):
            at_z = lax.rem(z + k, 8)
            for j in range(2):
                at = (yl ^ j) * 4 + lax.div(at_z, 2)
                full_window = lax.dynamic_update_slice(
                    full_window, block[j][None], (lax.rem(at_z, 2), 0, at * rows)
                )
        full_window = full_window.reshape(4 * CROWS, 8 * rows)

    with jax.named_scope("rows"):
        moved = mm(row_place, incoming_rows.reshape(-1, 3 * feats))

        def averaged(first, second):
            return ((first.astype(F32) + second) * 0.5).astype(BF)

        merged = (
            averaged(gate_first, moved[:, :feats]),
            averaged(up_first, moved[:, feats : 2 * feats]),
            averaged(down_first, moved[:, 2 * feats :]),
        )

    with jax.named_scope("correlation"):
        theirs = swapped(nt(full_window, full_chosen[units:]), "core")
        correlation = (nt(full_window, full_chosen[:units]) + theirs) * (1.0 / math.sqrt(16 * rows))
    return (*merged, correlation)


def solution(mesh):
    split = Mesh(mesh.devices.reshape(2, 8, 2, 2, 4), AXES)
    placed = (*(P(DP, MP),) * 7, P())
    return jax.shard_map(
        local,
        mesh=split,
        in_specs=placed,
        out_specs=(P(DP, MP), P(DP, MP), P(DP, MP), P(MP, DP)),
        check_vma=False,
    )
```

```python
import math

import jax
import jax.numpy as jnp
from jax import lax
from jax.sharding import Mesh
from jax.sharding import PartitionSpec as P

D = 5120
CROWS = 216
CAPACITY = 14
AXES = ("y_lo", "z", "core", "y_hi", "x")
DP = ("y_lo", "z", "core")
MP = ("y_hi", "x")
CHIPS = ("y_lo", "z")
BF = jnp.bfloat16
F32 = jnp.float32


def shifted(x, axis, k):
    n = lax.axis_size(axis)
    return lax.ppermute(x, axis, [(i, (i + k) % n) for i in range(n)])


def swapped(x, axis):
    return lax.ppermute(x, axis, [(0, 1), (1, 0)])


def ring(block, axis):
    n = lax.axis_size(axis)
    up = down = block
    found = [(0, block)]
    for k in range(1, n // 2):
        up = shifted(up, axis, 1)
        down = shifted(down, axis, -1)
        found += [(n - k, up), (k, down)]
    half = block.shape[0] // 2
    far = jnp.concatenate(
        [shifted(up[:half], axis, 1), shifted(down[half:], axis, -1)], axis=0
    )
    return [*found, (n // 2, far)]


def on_some(x, axes, pairs):
    flat = [(2 * a + b, 2 * c + d) for (a, b), (c, d) in pairs]
    return lax.ppermute(x, axes, flat)


def window_perm():
    def flat(yl, z, c, yh, x):
        return (((yl * 8 + z) * 2 + c) * 2 + yh) * 4 + x

    return [
        (flat(yl, z, c, yh, x), flat(yh, x * 2 + z % 2, c, yl, z // 2))
        for yl in range(2)
        for z in range(8)
        for c in range(2)
        for yh in range(2)
        for x in range(4)
    ]


def one_hot(index, size):
    return (index[:, None] == lax.broadcasted_iota(jnp.int32, (index.shape[0], size), 1)).astype(BF)


def mm(a, b):
    return jnp.dot(a, b, preferred_element_type=F32)


def nt(a, b):
    return lax.dot_general(a, b, (((1,), (1,)), ((), ())), preferred_element_type=F32)


def routes(matching, count, me, capacity):
    groups = matching.reshape(-1, count)
    number = groups.shape[0]
    owned = lax.div(groups, count) == me
    before = lax.broadcasted_iota(jnp.int32, (count, count), 0) < lax.broadcasted_iota(
        jnp.int32, (count, count), 1
    )
    before = before.astype(BF)
    rank = mm(owned.astype(BF), before).astype(jnp.int32)
    slots = jnp.arange(capacity, dtype=jnp.int32)
    picked = owned[:, None, :] & (rank[:, None, :] == slots[None, :, None])
    offsets = lax.rem(groups, count)
    send = jnp.sum(jnp.where(picked, offsets[:, None, :], 0), axis=2).reshape(-1)
    mine = lax.dynamic_slice_in_dim(matching, me * count, count)
    owner = lax.div(mine, count)
    from_block = owner[:, None] == lax.broadcasted_iota(jnp.int32, (count, number), 1)
    arrival = lax.dot_general(
        before, from_block.astype(BF), (((0,), (0,)), ((), ())), preferred_element_type=F32
    )
    arrival = jnp.sum(jnp.where(from_block, arrival, 0.0), axis=1).astype(jnp.int32)
    return one_hot(send, count), owner * capacity + arrival


def activated(pre, count):
    return (jax.nn.silu(pre[:count]) * pre[count:]).astype(BF)


def local(tokens, gate_first, up_first, down_first, gate_second, up_second, down_second, matching):
    units, feats = gate_first.shape
    yl, z, c, yh, x = (lax.axis_index(a) for a in AXES)
    chip = lax.axis_index(CHIPS)
    rows = tokens.shape[0]
    quarter = 4 * rows
    factor = 1.0 / math.sqrt(D)

    def put(held, block, *at):
        return lax.dynamic_update_slice(held, block, at)

    with jax.named_scope("tokens"):
        near_other = swapped(tokens, "y_lo")
        far_own = swapped(tokens, "y_hi")
        far_other = lax.ppermute(tokens, ("y_lo", "y_hi"), [(i, 3 - i) for i in range(4)])
        first_row = yl == 0
        pair = jnp.concatenate(
            [
                jnp.concatenate(
                    [jnp.where(first_row, own, other), jnp.where(first_row, other, own)], axis=0
                )
                for own, other in ((tokens, near_other), (far_own, far_other))
            ],
            axis=1,
        )

    pair, gate_first, up_first, gate_second, up_second, down_second, matching = lax.optimization_barrier(
        (pair, gate_first, up_first, gate_second, up_second, down_second, matching)
    )

    with jax.named_scope("weights"):
        pairs_far = [((0, 1), (0, 0)), ((1, 0), (1, 1))]
        pairs_core = [((0, 0), (1, 0)), ((1, 1), (0, 1))]
        keeps = c == yh

        def both_features(mine):
            far = on_some(mine, ("core", "y_hi"), pairs_far)
            near_shared = on_some(mine, ("core", "y_hi"), pairs_core)
            far_shared = on_some(far, ("core", "y_hi"), pairs_core)
            return jnp.concatenate(
                [jnp.where(keeps, mine, near_shared), jnp.where(keeps, far, far_shared)], axis=1
            )

        second_chip = both_features(jnp.concatenate([gate_second, up_second], axis=0))
        first_chip = both_features(jnp.concatenate([gate_first[:CROWS], up_first[:CROWS]], axis=0))

    with jax.named_scope("tokens"):
        held = jnp.zeros((16 * rows, 2 * feats), BF)
        for k, block in ring(pair, "z"):
            held = put(held, block, lax.rem(z + k, 8) * 2 * rows, 0)

    with jax.named_scope("routing"):
        row_send, row_land = routes(matching, units, 2 * chip + c, CAPACITY)
        act_send, act_land = routes(matching, units, 2 * chip + yh, CAPACITY)
        row_place = one_hot(row_land, 32 * CAPACITY)
        act_place = one_hot(act_land, 32 * CAPACITY)

    def exchanged(weights):
        total = None
        for dx in (2, 1, 3, 0):
            block = lax.dynamic_slice_in_dim(held, lax.rem(x + dx, 4) * quarter, quarter)
            term = (nt(weights, block) * factor).astype(BF)
            if dx:
                term = shifted(term, "x", dx)
            total = term.astype(F32) if total is None else total + term.astype(F32)
        return total

    with jax.named_scope("rows"):
        row_send, held = lax.optimization_barrier((row_send, held))
        outgoing_rows = mm(row_send, jnp.concatenate([gate_second, up_second], axis=1)).astype(BF)
        incoming_rows = lax.all_to_all(
            outgoing_rows.reshape(32, CAPACITY, 2 * feats), DP, split_axis=0, concat_axis=0, tiled=True
        )

    with jax.named_scope("first_sums"):
        hidden_first = activated(exchanged(first_chip), CROWS)

    with jax.named_scope("second_sums"):
        hidden_second = activated(exchanged(second_chip), units)
        outgoing = mm(act_send, hidden_second).astype(BF).reshape(32, CAPACITY, quarter)

    outgoing, hidden_first, incoming_rows = lax.optimization_barrier(
        (outgoing, hidden_first, incoming_rows)
    )

    with jax.named_scope("matched"):
        incoming = lax.all_to_all(
            outgoing, ("y_lo", "z", "y_hi"), split_axis=0, concat_axis=0, tiled=True
        )
        row_send, incoming = lax.optimization_barrier((row_send, incoming))
        chosen = mm(act_place, incoming.reshape(-1, quarter)).astype(BF)
        both = jnp.stack([chosen, swapped(chosen, "y_hi")])
        full_chosen = jnp.zeros((2, units, 4 * quarter), BF)
        for k, block in ring(both, "x"):
            for j in range(2):
                full_chosen = put(
                    full_chosen, block[j][None], yh ^ j ^ c, 0, lax.rem(x + k, 4) * quarter
                )

    with jax.named_scope("window"):
        window = lax.ppermute(hidden_first, AXES, window_perm())
        both = jnp.stack([window, swapped(window, "y_lo")])
        full_window = jnp.zeros((4, CROWS, 4 * quarter), BF)
        for k, block in ring(both, "z"):
            at_z = lax.rem(z + k, 8)
            for j in range(2):
                full_window = put(
                    full_window,
                    block[j][None],
                    2 * lax.rem(at_z, 2) + (yl ^ j),
                    0,
                    lax.div(at_z, 2) * quarter,
                )
        full_window = full_window.reshape(4 * CROWS, 4 * quarter)

    with jax.named_scope("rows"):
        outgoing_down = mm(row_send, down_second).astype(BF).reshape(32, CAPACITY, feats)
        incoming_down = lax.all_to_all(outgoing_down, DP, split_axis=0, concat_axis=0, tiled=True)
        full_window, incoming_down = lax.optimization_barrier((full_window, incoming_down))
        moved = mm(row_place, incoming_rows.reshape(-1, 2 * feats))
        moved_down = mm(row_place, incoming_down.reshape(-1, feats))

        def averaged(first, second):
            return ((first.astype(F32) + second) * 0.5).astype(BF)

        merged = (
            averaged(gate_first, moved[:, :feats]),
            averaged(up_first, moved[:, feats:]),
            averaged(down_first, moved_down),
        )

    with jax.named_scope("correlation"):
        theirs = swapped(nt(full_window, full_chosen[1]), "core")
        correlation = (nt(full_window, full_chosen[0]) + theirs) * (1.0 / math.sqrt(32 * rows))
    return (*merged, correlation)


def solution(mesh):
    split = Mesh(mesh.devices.reshape(2, 8, 2, 2, 4), AXES)
    placed = (*(P(DP, MP),) * 7, P())
    return jax.shard_map(
        local,
        mesh=split,
        in_specs=placed,
        out_specs=(P(DP, MP), P(DP, MP), P(DP, MP), P(MP, DP)),
        check_vma=False,
    )
```

```python
import functools
import math

import jax
import jax.numpy as jnp
from jax import lax
from jax.experimental import pallas as pl
from jax.experimental.pallas import tpu as pltpu
from jax.sharding import Mesh
from jax.sharding import PartitionSpec as P

D = 5120
CROWS = 216
CAPACITY = 14
AXES = ("y_lo", "z", "core", "y_hi", "x")
DP = ("y_lo", "z", "core")
MP = ("y_hi", "x")
CHIPS = ("y_lo", "z")
BF = jnp.bfloat16
F32 = jnp.float32


def shifted(x, axis, k):
    n = lax.axis_size(axis)
    return lax.ppermute(x, axis, [(i, (i + k) % n) for i in range(n)])


def swapped(x, axis):
    return lax.ppermute(x, axis, [(0, 1), (1, 0)])


def ring(block, axis, cut):
    n = lax.axis_size(axis)
    up = down = block
    ups, downs = [], []
    for _ in range(1, n // 2):
        up = shifted(up, axis, 1)
        down = shifted(down, axis, -1)
        ups.append(up)
        downs.append(down)
    far = [shifted(up[:cut], axis, 1), shifted(down[cut:], axis, -1)]
    return [block, *downs, *far, *ups[::-1]]


def on_some(x, axes, pairs):
    flat = [(2 * a + b, 2 * c + d) for (a, b), (c, d) in pairs]
    return lax.ppermute(x, axes, flat)


def window_perm():
    def flat(yl, z, c, yh, x):
        return (((yl * 8 + z) * 2 + c) * 2 + yh) * 4 + x

    return [
        (flat(yl, z, c, yh, x), flat(yh, x * 2 + z % 2, c, yl, z // 2))
        for yl in range(2)
        for z in range(8)
        for c in range(2)
        for yh in range(2)
        for x in range(4)
    ]


def one_hot(index, size):
    return (index[:, None] == lax.broadcasted_iota(jnp.int32, (index.shape[0], size), 1)).astype(BF)


def mm(a, b):
    return jnp.dot(a, b, preferred_element_type=F32)


def nt(a, b):
    return lax.dot_general(a, b, (((1,), (1,)), ((), ())), preferred_element_type=F32)


def routes(matching, count, me, capacity):
    groups = matching.reshape(-1, count)
    number = groups.shape[0]
    owned = lax.div(groups, count) == me
    before = lax.broadcasted_iota(jnp.int32, (count, count), 0) < lax.broadcasted_iota(
        jnp.int32, (count, count), 1
    )
    before = before.astype(BF)
    rank = mm(owned.astype(BF), before).astype(jnp.int32)
    slots = jnp.arange(capacity, dtype=jnp.int32)
    picked = owned[:, None, :] & (rank[:, None, :] == slots[None, :, None])
    offsets = lax.rem(groups, count)
    send = jnp.sum(jnp.where(picked, offsets[:, None, :], 0), axis=2).reshape(-1)
    mine = lax.dynamic_slice_in_dim(matching, me * count, count)
    owner = lax.div(mine, count)
    from_block = owner[:, None] == lax.broadcasted_iota(jnp.int32, (count, number), 1)
    arrival = lax.dot_general(
        before, from_block.astype(BF), (((0,), (0,)), ((), ())), preferred_element_type=F32
    )
    arrival = jnp.sum(jnp.where(from_block, arrival, 0.0), axis=1).astype(jnp.int32)
    return one_hot(send, count), owner * capacity + arrival


def ring_pieces(n):
    half = n // 2
    return [(k, False) for k in range(half + 1)] + [(k, k == half) for k in range(half, n)]


def terms_kernel(factor, place_ref, *refs):
    pieces, (near, far), outs, held = refs[:9], refs[9:11], refs[11:15], refs[15]
    z, x = place_ref[0], place_ref[1]
    rows = held.shape[1]
    for (k, second), piece in zip(ring_pieces(8), pieces):
        at = lax.rem(z + k, 8)
        start = rows - piece.shape[0] if second else 0
        held[at, start : start + piece.shape[0]] = piece[...]
    feats = near.shape[1]
    for dx, out in enumerate(outs):
        first = 2 * lax.rem(x + dx, 4)
        for half in range(2):
            block = held[first + half]
            total = nt(near[...], block[:, :feats]) + nt(far[...], block[:, feats:])
            out[:, half * rows : (half + 1) * rows] = (total * factor).astype(BF)


def products_kernel(place_ref, *refs):
    windows, seconds, own, theirs = refs[:9], refs[9:14], refs[14], refs[15]
    held_window, held_second = refs[16:]
    z, x, flip = place_ref[0], place_ref[1], place_ref[2]
    height = held_window.shape[1] // 2
    for (k, second), piece in zip(ring_pieces(8), windows):
        at = lax.rem(z + k, 8)
        start = height - piece.shape[0] if second else 0
        row = pl.multiple_of(lax.rem(at, 2) * height + start, 16)
        held_window[lax.div(at, 2), pl.ds(row, piece.shape[0])] = piece[...]
    for (k, second), piece in zip(ring_pieces(4), seconds):
        for j in range(piece.shape[0]):
            held_second[lax.rem(x + k, 4), flip ^ (1 if second else j)] = piece[j]
    for slot, out in enumerate((own, theirs)):
        total = None
        for at in range(4):
            part = nt(held_second[at, slot], held_window[at])
            total = part if total is None else total + part
        out[...] = total


def in_vmem(kernel, shapes, scratch, place, *arrays):
    vmem = pl.BlockSpec(memory_space=pltpu.VMEM)
    return pl.pallas_call(
        kernel,
        out_shape=shapes,
        in_specs=[pl.BlockSpec(memory_space=pltpu.SMEM)] + [vmem] * len(arrays),
        out_specs=[vmem] * len(shapes),
        scratch_shapes=scratch,
        compiler_params=pltpu.CompilerParams(vmem_limit_bytes=24 << 20),
    )(place, *arrays)


def activated(pre, count):
    return (jax.nn.silu(pre[:count]) * pre[count:]).astype(BF)


def local(tokens, gate_first, up_first, down_first, gate_second, up_second, down_second, matching):
    units, feats = gate_first.shape
    yl, z, c, yh, x = (lax.axis_index(a) for a in AXES)
    chip = lax.axis_index(CHIPS)
    rows = tokens.shape[0]
    quarter = 4 * rows
    factor = 1.0 / math.sqrt(D)

    with jax.named_scope("tokens"):
        near_other = swapped(tokens, "y_lo")
        far_own = swapped(tokens, "y_hi")
        far_other = lax.ppermute(tokens, ("y_lo", "y_hi"), [(i, 3 - i) for i in range(4)])
        first_row = yl == 0
        pair = jnp.concatenate(
            [
                jnp.concatenate(
                    [jnp.where(first_row, own, other), jnp.where(first_row, other, own)], axis=0
                )
                for own, other in ((tokens, near_other), (far_own, far_other))
            ],
            axis=1,
        )

    with jax.named_scope("weights"):
        mine = jnp.concatenate([gate_second, up_second, gate_first[:CROWS], up_first[:CROWS]], axis=0)

    pair, mine, gate_second, up_second, down_second, matching = lax.optimization_barrier(
        (pair, mine, gate_second, up_second, down_second, matching)
    )

    with jax.named_scope("weights"):
        pairs_far = [((0, 1), (0, 0)), ((1, 0), (1, 1))]
        pairs_core = [((0, 0), (1, 0)), ((1, 1), (0, 1))]
        keeps = c == yh

        def both_features(mine):
            far = on_some(mine, ("core", "y_hi"), pairs_far)
            near_shared = on_some(mine, ("core", "y_hi"), pairs_core)
            far_shared = on_some(far, ("core", "y_hi"), pairs_core)
            return jnp.where(keeps, mine, near_shared), jnp.where(keeps, far, far_shared)

        near, far = both_features(mine)

    with jax.named_scope("tokens"):
        blocks = ring(pair, "z", rows)

    with jax.named_scope("routing"):
        row_send, row_land = routes(matching, units, 2 * chip + c, CAPACITY)
        act_send, act_land = routes(matching, units, 2 * chip + yh, CAPACITY)
        row_place = one_hot(row_land, 32 * CAPACITY)
        act_place = one_hot(act_land, 32 * CAPACITY)

    with jax.named_scope("rows"):
        row_send, blocks = lax.optimization_barrier((row_send, blocks))
        outgoing_rows = mm(row_send, jnp.concatenate([gate_second, up_second], axis=1)).astype(BF)
        incoming_rows = lax.all_to_all(
            outgoing_rows.reshape(32, CAPACITY, 2 * feats), DP, split_axis=0, concat_axis=0, tiled=True
        )

    with jax.named_scope("sums"):
        parts = in_vmem(
            functools.partial(terms_kernel, factor),
            [jax.ShapeDtypeStruct((near.shape[0], quarter), BF)] * 4,
            [pltpu.VMEM((8, 2 * rows, 2 * feats), BF)],
            jnp.stack([z, x]),
            *blocks,
            near,
            far,
        )
        total = parts[0].astype(F32)
        for dx in (2, 1, 3):
            total = total + shifted(parts[dx], "x", dx).astype(F32)
        hidden_second = activated(total[: 2 * units], units)
        hidden_first = activated(total[2 * units :], CROWS)
        outgoing = mm(act_send, hidden_second).astype(BF).reshape(32, CAPACITY, quarter)

    outgoing, hidden_first, incoming_rows = lax.optimization_barrier(
        (outgoing, hidden_first, incoming_rows)
    )

    with jax.named_scope("matched"):
        incoming = lax.all_to_all(
            outgoing, ("y_lo", "z", "y_hi"), split_axis=0, concat_axis=0, tiled=True
        )
        row_send, incoming = lax.optimization_barrier((row_send, incoming))
        chosen = mm(act_place, incoming.reshape(-1, quarter)).astype(BF)
        both = jnp.stack([chosen, swapped(chosen, "y_hi")])
        seconds = ring(both, "x", 1)

    with jax.named_scope("window"):
        window = lax.ppermute(hidden_first, AXES, window_perm())
        other = swapped(window, "y_lo")
        both = jnp.concatenate(
            [jnp.where(first_row, window, other), jnp.where(first_row, other, window)], axis=0
        )
        windows = ring(both, "z", 224)

    with jax.named_scope("rows"):
        outgoing_down = mm(row_send, down_second).astype(BF).reshape(32, CAPACITY, feats)
        incoming_down = lax.all_to_all(outgoing_down, DP, split_axis=0, concat_axis=0, tiled=True)
        windows, incoming_down = lax.optimization_barrier((windows, incoming_down))
        moved = mm(row_place, incoming_rows.reshape(-1, 2 * feats))
        moved_down = mm(row_place, incoming_down.reshape(-1, feats))

        def averaged(first, second):
            return ((first.astype(F32) + second) * 0.5).astype(BF)

        merged = (
            averaged(gate_first, moved[:, :feats]),
            averaged(up_first, moved[:, feats:]),
            averaged(down_first, moved_down),
        )

    with jax.named_scope("correlation"):
        own, theirs = in_vmem(
            products_kernel,
            [jax.ShapeDtypeStruct((units, 4 * CROWS), F32)] * 2,
            [
                pltpu.VMEM((4, 4 * CROWS, quarter), BF),
                pltpu.VMEM((4, 2, units, quarter), BF),
            ],
            jnp.stack([z, x, yh ^ c]),
            *windows,
            *seconds,
        )
        correlation = ((own + swapped(theirs, "core")) * (1.0 / math.sqrt(32 * rows))).T
    return (*merged, correlation)


def solution(mesh):
    split = Mesh(mesh.devices.reshape(2, 8, 2, 2, 4), AXES)
    placed = (*(P(DP, MP),) * 7, P())
    return jax.shard_map(
        local,
        mesh=split,
        in_specs=placed,
        out_specs=(P(DP, MP), P(DP, MP), P(DP, MP), P(MP, DP)),
        check_vma=False,
    )
```

```python
import functools
import math

import jax
import jax.numpy as jnp
from jax import lax
from jax.experimental import pallas as pl
from jax.experimental.pallas import tpu as pltpu
from jax.sharding import Mesh
from jax.sharding import PartitionSpec as P

D = 5120
CROWS = 216
CAPACITY = 16
AXES = ("y_lo", "z", "core", "y_hi", "x")
DP = ("y_lo", "z", "core")
MP = ("y_hi", "x")
CHIPS = ("y_lo", "z")
BF = jnp.bfloat16
F32 = jnp.float32


def shifted(x, axis, k):
    n = lax.axis_size(axis)
    return lax.ppermute(x, axis, [(i, (i + k) % n) for i in range(n)])


def swapped(x, axis):
    return lax.ppermute(x, axis, [(0, 1), (1, 0)])


def ring(block, axis, cut):
    n = lax.axis_size(axis)
    up = down = block
    ups, downs = [], []
    for _ in range(1, n // 2):
        up, down = lax.optimization_barrier((shifted(up, axis, 1), shifted(down, axis, -1)))
        ups.append(up)
        downs.append(down)
    far = [shifted(up[:cut], axis, 1), shifted(down[cut:], axis, -1)]
    return [block, *downs, *far, *ups[::-1]]


def on_some(x, axes, pairs):
    flat = [(2 * a + b, 2 * c + d) for (a, b), (c, d) in pairs]
    return lax.ppermute(x, axes, flat)


def window_perm():
    def flat(yl, z, c, yh, x):
        return (((yl * 8 + z) * 2 + c) * 2 + yh) * 4 + x

    return [
        (flat(yl, z, c, yh, x), flat(yh, x * 2 + z % 2, c, yl, z // 2))
        for yl in range(2)
        for z in range(8)
        for c in range(2)
        for yh in range(2)
        for x in range(4)
    ]


def one_hot(index, size):
    return (index[:, None] == lax.broadcasted_iota(jnp.int32, (index.shape[0], size), 1)).astype(BF)


def mm(a, b):
    return jnp.dot(a, b, preferred_element_type=F32)


def nt(a, b):
    return lax.dot_general(a, b, (((1,), (1,)), ((), ())), preferred_element_type=F32)


def routes(matching, count, me, capacity):
    groups = matching.reshape(-1, count)
    number = groups.shape[0]
    owned = lax.div(groups, count) == me
    before = lax.broadcasted_iota(jnp.int32, (count, count), 0) < lax.broadcasted_iota(
        jnp.int32, (count, count), 1
    )
    before = before.astype(BF)
    rank = mm(owned.astype(BF), before).astype(jnp.int32)
    slots = jnp.arange(capacity, dtype=jnp.int32)
    picked = owned[:, None, :] & (rank[:, None, :] == slots[None, :, None])
    offsets = lax.rem(groups, count)
    send = jnp.sum(jnp.where(picked, offsets[:, None, :], 0), axis=2).reshape(-1)
    mine = lax.dynamic_slice_in_dim(matching, me * count, count)
    owner = lax.div(mine, count)
    from_block = owner[:, None] == lax.broadcasted_iota(jnp.int32, (count, number), 1)
    arrival = lax.dot_general(
        before, from_block.astype(BF), (((0,), (0,)), ((), ())), preferred_element_type=F32
    )
    arrival = jnp.sum(jnp.where(from_block, arrival, 0.0), axis=1).astype(jnp.int32)
    return one_hot(send, count), owner * capacity + arrival


def ring_pieces(n):
    half = n // 2
    return [(k, False) for k in range(half + 1)] + [(k, k == half) for k in range(half, n)]


def terms_kernel(factor, place_ref, *refs):
    pieces, (mine, near_shared, far_mine, far_shared) = refs[:9], refs[9:13]
    outs, (held, weights, made, arrived, left) = refs[13:21], refs[21:]
    z, x, keeps = place_ref[0], place_ref[1], place_ref[2]
    block_rows = held.shape[1] // 2
    copies = []
    for (k, second), piece in zip(ring_pieces(8), pieces):
        at = lax.rem(z + k, 8)
        count = piece.shape[0]
        row = lax.rem(at, 2) * block_rows + (block_rows - count if second else 0)
        place = held.at[lax.div(at, 2), pl.ds(pl.multiple_of(row, 16), count)]
        copies.append(pltpu.make_async_copy(piece, place, arrived.at[len(copies)]))
        copies[-1].start()
    for slot, (own, shared) in enumerate(((mine, near_shared), (far_mine, far_shared))):
        from_own = pltpu.make_async_copy(own, weights.at[slot], arrived.at[9 + slot])
        from_shared = pltpu.make_async_copy(shared, weights.at[slot], arrived.at[9 + slot])
        pl.when(keeps == 1)(from_own.start)
        pl.when(keeps == 0)(from_shared.start)
        copies.append(from_own)
    for copy in copies:
        copy.wait()
    feats = weights.shape[2]
    split = outs[4].shape[0]
    sent = []
    for group, rows in ((0, slice(split, None)), (1, slice(0, split))):
        for dx in (2, 1, 3, 0):
            block = held[lax.rem(x + dx, 4)]
            total = nt(weights[0, rows], block[:, :feats]) + nt(weights[1, rows], block[:, feats:])
            made[dx, rows] = (total * factor).astype(BF)
            out = outs[4 * group + dx]
            sent.append(pltpu.make_async_copy(made.at[dx, rows], out, left.at[4 * group + dx]))
            sent[-1].start()
    for copy in sent:
        copy.wait()


def products_kernel(place_ref, *refs):
    windows, seconds, outs = refs[:9], refs[9:14], refs[14:16]
    held_window, held_second, made, arrived, left = refs[16:]
    z, x, flip = place_ref[0], place_ref[1], place_ref[2]
    height = held_window.shape[1] // 2
    copies = []

    def fetched(piece, place):
        copies.append(pltpu.make_async_copy(piece, place, arrived.at[len(copies)]))
        copies[-1].start()

    for (k, second), piece in zip(ring_pieces(8), windows):
        at = lax.rem(z + k, 8)
        count = piece.shape[0]
        row = lax.rem(at, 2) * height + (height - count if second else 0)
        fetched(piece, held_window.at[lax.div(at, 2), pl.ds(pl.multiple_of(row, 16), count)])
    for (k, second), piece in zip(ring_pieces(4), seconds):
        for j in range(piece.shape[0]):
            slot = flip ^ 1 if second or j else flip
            fetched(piece.at[j], held_second.at[lax.rem(x + k, 4), slot])
    for copy in copies:
        copy.wait()
    sent = []
    for slot in (1, 0):
        total = None
        for at in range(4):
            part = nt(held_second[at, slot], held_window[at])
            total = part if total is None else total + part
        made[slot] = total
        sent.append(pltpu.make_async_copy(made.at[slot], outs[slot], left.at[slot]))
        sent[-1].start()
    for copy in sent:
        copy.wait()


def on_device(kernel, shapes, scratch, place, *arrays):
    anywhere = pl.BlockSpec(memory_space=pl.ANY)
    return pl.pallas_call(
        kernel,
        out_shape=shapes,
        in_specs=[pl.BlockSpec(memory_space=pltpu.SMEM)] + [anywhere] * len(arrays),
        out_specs=[anywhere] * len(shapes),
        scratch_shapes=scratch,
        compiler_params=pltpu.CompilerParams(vmem_limit_bytes=24 << 20),
    )(place, *arrays)


def activated(pre, count):
    return (jax.nn.silu(pre[:count]) * pre[count:]).astype(BF)


def local(tokens, gate_first, up_first, down_first, gate_second, up_second, down_second, matching):
    units, feats = gate_first.shape
    yl, z, c, yh, x = (lax.axis_index(a) for a in AXES)
    chip = lax.axis_index(CHIPS)
    rows = tokens.shape[0]
    quarter = 4 * rows
    factor = 1.0 / math.sqrt(D)

    with jax.named_scope("tokens"):
        near_other = swapped(tokens, "y_lo")
        far_own = swapped(tokens, "y_hi")
        far_other = lax.ppermute(tokens, ("y_lo", "y_hi"), [(i, 3 - i) for i in range(4)])
        first_row = yl == 0
        pair = jnp.concatenate(
            [
                jnp.concatenate(
                    [jnp.where(first_row, own, other), jnp.where(first_row, other, own)], axis=0
                )
                for own, other in ((tokens, near_other), (far_own, far_other))
            ],
            axis=1,
        )

    with jax.named_scope("weights"):
        mine = jnp.concatenate([gate_second, up_second, gate_first[:CROWS], up_first[:CROWS]], axis=0)

    pair, mine, gate_second, up_second, down_second, matching = lax.optimization_barrier(
        (pair, mine, gate_second, up_second, down_second, matching)
    )

    with jax.named_scope("tokens"):
        blocks = ring(pair, "z", rows)

    with jax.named_scope("weights"):
        keeps = c == yh
        pairs_far = [((0, 1), (0, 0)), ((1, 0), (1, 1))]
        pairs_core = [((0, 0), (1, 0)), ((1, 1), (0, 1))]
        near_shared = on_some(mine, ("core", "y_hi"), pairs_core)
        far = on_some(mine, ("core", "y_hi"), pairs_far)
        far, _ = lax.optimization_barrier((far, blocks[3]))
        far_shared = on_some(far, ("core", "y_hi"), pairs_core)
        weights = (mine, near_shared, far, far_shared)

    with jax.named_scope("routing"):
        row_send, row_land = routes(matching, units, 2 * chip + c, CAPACITY)
        act_send, act_land = routes(matching, units, 2 * chip + yh, CAPACITY)
        row_place = one_hot(row_land, 32 * CAPACITY)
        act_place = one_hot(act_land, 32 * CAPACITY)

    with jax.named_scope("rows"):
        row_send, _ = lax.optimization_barrier((row_send, blocks[1]))
        second_rows = jnp.concatenate([gate_second, up_second, down_second], axis=1)
        outgoing_rows = mm(row_send, second_rows).astype(BF).reshape(32, CAPACITY, 3 * feats)
        outgoing_rows, _ = lax.optimization_barrier((outgoing_rows, blocks[2]))
        incoming_rows = lax.all_to_all(outgoing_rows, DP, split_axis=0, concat_axis=0, tiled=True)

    with jax.named_scope("sums"):
        first_parts = [jax.ShapeDtypeStruct((2 * CROWS, quarter), BF)] * 4
        second_parts = [jax.ShapeDtypeStruct((2 * units, quarter), BF)] * 4
        parts = on_device(
            functools.partial(terms_kernel, factor),
            [*first_parts, *second_parts],
            [
                pltpu.VMEM((4, 4 * rows, 2 * feats), BF),
                pltpu.VMEM((2, *mine.shape), BF),
                pltpu.VMEM((4, mine.shape[0], quarter), BF),
                pltpu.SemaphoreType.DMA((11,)),
                pltpu.SemaphoreType.DMA((8,)),
            ],
            jnp.stack([z, x, keeps.astype(jnp.int32)]),
            *blocks,
            *weights,
        )

        def summed(terms):
            total = terms[0].astype(F32)
            for dx in (2, 1, 3):
                total = total + shifted(terms[dx], "x", dx).astype(F32)
            return total

        hidden_first = activated(summed(parts[:4]), CROWS)
        hidden_second = activated(summed(parts[4:]), units)
        act_send, _ = lax.optimization_barrier((act_send, incoming_rows))
        outgoing = mm(act_send, hidden_second).astype(BF).reshape(32, CAPACITY, quarter)

    with jax.named_scope("rows"):
        moved = mm(row_place, incoming_rows.reshape(-1, 3 * feats))

        def averaged(first, second):
            return ((first.astype(F32) + second) * 0.5).astype(BF)

        merged = (
            averaged(gate_first, moved[:, :feats]),
            averaged(up_first, moved[:, feats : 2 * feats]),
            averaged(down_first, moved[:, 2 * feats :]),
        )

    with jax.named_scope("window"):
        window = lax.ppermute(hidden_first, AXES, window_perm())
        other = swapped(window, "y_lo")
        both = jnp.concatenate(
            [jnp.where(first_row, window, other), jnp.where(first_row, other, window)], axis=0
        )
        both, _ = lax.optimization_barrier((both, outgoing))
        windows = ring(both, "z", 224)

    with jax.named_scope("matched"):
        incoming = lax.all_to_all(
            outgoing, ("y_lo", "z", "y_hi"), split_axis=0, concat_axis=0, tiled=True
        )
        act_place, merged, _ = lax.optimization_barrier((act_place, merged, windows[2]))
        chosen = mm(act_place, incoming.reshape(-1, quarter)).astype(BF)
        both = jnp.stack([chosen, swapped(chosen, "y_hi")])
        seconds = ring(both, "x", 1)

    with jax.named_scope("correlation"):
        own, theirs = on_device(
            products_kernel,
            [jax.ShapeDtypeStruct((units, 4 * CROWS), F32)] * 2,
            [
                pltpu.VMEM((4, 4 * CROWS, quarter), BF),
                pltpu.VMEM((4, 2, units, quarter), BF),
                pltpu.VMEM((2, units, 4 * CROWS), F32),
                pltpu.SemaphoreType.DMA((17,)),
                pltpu.SemaphoreType.DMA((2,)),
            ],
            jnp.stack([z, x, yh ^ c]),
            *windows,
            *seconds,
        )
        correlation = ((own + swapped(theirs, "core")) * (1.0 / math.sqrt(32 * rows))).T
    return (*merged, correlation)


def solution(mesh):
    split = Mesh(mesh.devices.reshape(2, 8, 2, 2, 4), AXES)
    placed = (*(P(DP, MP),) * 7, P())
    return jax.shard_map(
        local,
        mesh=split,
        in_specs=placed,
        out_specs=(P(DP, MP), P(DP, MP), P(DP, MP), P(MP, DP)),
        check_vma=False,
    )
```

```python
import functools
import math

import jax
import jax.numpy as jnp
from jax import lax
from jax.experimental import pallas as pl
from jax.experimental.pallas import tpu as pltpu
from jax.sharding import Mesh
from jax.sharding import PartitionSpec as P

D = 5120
CROWS = 216
CAPACITY = 16
AXES = ("y_lo", "z", "core", "y_hi", "x")
DP = ("y_lo", "z", "core")
MP = ("y_hi", "x")
CHIPS = ("y_lo", "z")
BF = jnp.bfloat16
F32 = jnp.float32


def shifted(x, axis, k):
    n = lax.axis_size(axis)
    return lax.ppermute(x, axis, [(i, (i + k) % n) for i in range(n)])


def swapped(x, axis):
    return lax.ppermute(x, axis, [(0, 1), (1, 0)])


def ring(block, axis, cut):
    n = lax.axis_size(axis)
    up = down = block
    ups, downs = [], []
    for _ in range(1, n // 2):
        up, down = lax.optimization_barrier((shifted(up, axis, 1), shifted(down, axis, -1)))
        ups.append(up)
        downs.append(down)
    up, down = lax.optimization_barrier((up[:cut], down[cut:]))
    far = [shifted(up, axis, 1), shifted(down, axis, -1)]
    return [block, *downs, *far, *ups[::-1]]


def on_some(x, axes, pairs):
    flat = [(2 * a + b, 2 * c + d) for (a, b), (c, d) in pairs]
    return lax.ppermute(x, axes, flat)


def window_perm():
    def flat(yl, z, c, yh, x):
        return (((yl * 8 + z) * 2 + c) * 2 + yh) * 4 + x

    return [
        (flat(yl, z, c, yh, x), flat(yh, x * 2 + z % 2, c, yl, z // 2))
        for yl in range(2)
        for z in range(8)
        for c in range(2)
        for yh in range(2)
        for x in range(4)
    ]


def one_hot(index, size):
    return (index[:, None] == lax.broadcasted_iota(jnp.int32, (index.shape[0], size), 1)).astype(BF)


def mm(a, b):
    return jnp.dot(a, b, preferred_element_type=F32)


def nt(a, b):
    return lax.dot_general(a, b, (((1,), (1,)), ((), ())), preferred_element_type=F32)


def routes(matching, count, me, capacity):
    groups = matching.reshape(-1, count)
    number = groups.shape[0]
    owned = lax.div(groups, count) == me
    before = lax.broadcasted_iota(jnp.int32, (count, count), 0) < lax.broadcasted_iota(
        jnp.int32, (count, count), 1
    )
    before = before.astype(BF)
    rank = mm(owned.astype(BF), before).astype(jnp.int32)
    slots = jnp.arange(capacity, dtype=jnp.int32)
    picked = owned[:, None, :] & (rank[:, None, :] == slots[None, :, None])
    offsets = lax.rem(groups, count)
    send = jnp.sum(jnp.where(picked, offsets[:, None, :], 0), axis=2).reshape(-1)
    mine = lax.dynamic_slice_in_dim(matching, me * count, count)
    owner = lax.div(mine, count)
    from_block = owner[:, None] == lax.broadcasted_iota(jnp.int32, (count, number), 1)
    arrival = lax.dot_general(
        before, from_block.astype(BF), (((0,), (0,)), ((), ())), preferred_element_type=F32
    )
    arrival = jnp.sum(jnp.where(from_block, arrival, 0.0), axis=1).astype(jnp.int32)
    return one_hot(send, count), owner * capacity + arrival


def ring_pieces(n):
    half = n // 2
    return [(k, False) for k in range(half + 1)] + [(k, k == half) for k in range(half, n)]


def terms_kernel(factor, place_ref, *refs):
    pieces, (mine, near_shared, far_mine, far_shared) = refs[:9], refs[9:13]
    outs, (held, weights, made, arrived, left) = refs[13:21], refs[21:]
    z, x, keeps = place_ref[0], place_ref[1], place_ref[2]
    block_rows = held.shape[1] // 2
    copies = []
    for (k, second), piece in zip(ring_pieces(8), pieces):
        at = lax.rem(z + k, 8)
        count = piece.shape[0]
        row = lax.rem(at, 2) * block_rows + (block_rows - count if second else 0)
        place = held.at[lax.div(at, 2), pl.ds(pl.multiple_of(row, 16), count)]
        copies.append(pltpu.make_async_copy(piece, place, arrived.at[len(copies)]))
        copies[-1].start()
    for slot, (own, shared) in enumerate(((mine, near_shared), (far_mine, far_shared))):
        from_own = pltpu.make_async_copy(own, weights.at[slot], arrived.at[9 + slot])
        from_shared = pltpu.make_async_copy(shared, weights.at[slot], arrived.at[9 + slot])
        pl.when(keeps == 1)(from_own.start)
        pl.when(keeps == 0)(from_shared.start)
        copies.append(from_own)
    for copy in copies:
        copy.wait()
    feats = weights.shape[2]
    split = outs[4].shape[0]
    sent = []
    for group, rows in ((0, slice(split, None)), (1, slice(0, split))):
        for dx in (2, 1, 3, 0):
            block = held[lax.rem(x + dx, 4)]
            total = nt(weights[0, rows], block[:, :feats]) + nt(weights[1, rows], block[:, feats:])
            made[dx, rows] = (total * factor).astype(BF)
            out = outs[4 * group + dx]
            sent.append(pltpu.make_async_copy(made.at[dx, rows], out, left.at[4 * group + dx]))
            sent[-1].start()
    for copy in sent:
        copy.wait()


def products_kernel(place_ref, *refs):
    windows, seconds, outs = refs[:9], refs[9:19], refs[19:21]
    held_window, held_second, made, arrived, left = refs[21:]
    z, x, flip = place_ref[0], place_ref[1], place_ref[2]
    height = held_window.shape[1] // 2
    copies = []

    def fetched(piece, place):
        copies.append(pltpu.make_async_copy(piece, place, arrived.at[len(copies)]))
        copies[-1].start()

    for (k, second), piece in zip(ring_pieces(8), windows):
        at = lax.rem(z + k, 8)
        count = piece.shape[0]
        row = lax.rem(at, 2) * height + (height - count if second else 0)
        fetched(piece, held_window.at[lax.div(at, 2), pl.ds(pl.multiple_of(row, 16), count)])
    for j in range(2):
        for (k, second), piece in zip(ring_pieces(4), seconds[5 * j : 5 * j + 5]):
            count = piece.shape[0]
            start = held_second.shape[2] - count if second else 0
            slot = flip ^ 1 if j else flip
            fetched(piece, held_second.at[lax.rem(x + k, 4), slot, pl.ds(start, count)])
    for copy in copies:
        copy.wait()
    sent = []
    for slot in (1, 0):
        total = None
        for at in range(4):
            part = nt(held_second[at, slot], held_window[at])
            total = part if total is None else total + part
        made[slot] = total
        sent.append(pltpu.make_async_copy(made.at[slot], outs[slot], left.at[slot]))
        sent[-1].start()
    for copy in sent:
        copy.wait()


def on_device(kernel, shapes, scratch, place, *arrays):
    anywhere = pl.BlockSpec(memory_space=pl.ANY)
    return pl.pallas_call(
        kernel,
        out_shape=shapes,
        in_specs=[pl.BlockSpec(memory_space=pltpu.SMEM)] + [anywhere] * len(arrays),
        out_specs=[anywhere] * len(shapes),
        scratch_shapes=scratch,
        compiler_params=pltpu.CompilerParams(vmem_limit_bytes=24 << 20),
    )(place, *arrays)


def activated(pre, count):
    return (jax.nn.silu(pre[:count]) * pre[count:]).astype(BF)


def local(tokens, gate_first, up_first, down_first, gate_second, up_second, down_second, matching):
    units, feats = gate_first.shape
    yl, z, c, yh, x = (lax.axis_index(a) for a in AXES)
    chip = lax.axis_index(CHIPS)
    rows = tokens.shape[0]
    quarter = 4 * rows
    factor = 1.0 / math.sqrt(D)

    with jax.named_scope("tokens"):
        near_other = swapped(tokens, "y_lo")
        far_own = swapped(tokens, "y_hi")
        far_other = lax.ppermute(tokens, ("y_lo", "y_hi"), [(i, 3 - i) for i in range(4)])
        first_row = yl == 0
        pair = jnp.concatenate(
            [
                jnp.concatenate(
                    [jnp.where(first_row, own, other), jnp.where(first_row, other, own)], axis=0
                )
                for own, other in ((tokens, near_other), (far_own, far_other))
            ],
            axis=1,
        )

    with jax.named_scope("weights"):
        mine = jnp.concatenate([gate_second, up_second, gate_first[:CROWS], up_first[:CROWS]], axis=0)

    pair, mine, gate_second, up_second, down_second, matching = lax.optimization_barrier(
        (pair, mine, gate_second, up_second, down_second, matching)
    )

    with jax.named_scope("tokens"):
        blocks = ring(pair, "z", rows)

    with jax.named_scope("weights"):
        keeps = c == yh
        pairs_far = [((0, 1), (0, 0)), ((1, 0), (1, 1))]
        pairs_core = [((0, 0), (1, 0)), ((1, 1), (0, 1))]
        near_shared = on_some(mine, ("core", "y_hi"), pairs_core)
        far = on_some(mine, ("core", "y_hi"), pairs_far)
        far, _ = lax.optimization_barrier((far, blocks[3]))
        far_shared = on_some(far, ("core", "y_hi"), pairs_core)
        weights = (mine, near_shared, far, far_shared)

    with jax.named_scope("routing"):
        row_send, row_land = routes(matching, units, 2 * chip + c, CAPACITY)
        act_send, act_land = routes(matching, units, 2 * chip + yh, CAPACITY)
        row_place = one_hot(row_land, 32 * CAPACITY)
        act_place = one_hot(act_land, 32 * CAPACITY)

    with jax.named_scope("rows"):
        row_send, _ = lax.optimization_barrier((row_send, blocks[1]))
        second_rows = jnp.concatenate([gate_second, up_second, down_second], axis=1)
        outgoing_rows = mm(row_send, second_rows).astype(BF).reshape(32, CAPACITY, 3 * feats)
        outgoing_rows, _ = lax.optimization_barrier((outgoing_rows, blocks[4:6]))
        incoming_rows = lax.all_to_all(outgoing_rows, DP, split_axis=0, concat_axis=0, tiled=True)

    with jax.named_scope("sums"):
        first_parts = [jax.ShapeDtypeStruct((2 * CROWS, quarter), BF)] * 4
        second_parts = [jax.ShapeDtypeStruct((2 * units, quarter), BF)] * 4
        parts = on_device(
            functools.partial(terms_kernel, factor),
            [*first_parts, *second_parts],
            [
                pltpu.VMEM((4, 4 * rows, 2 * feats), BF),
                pltpu.VMEM((2, *mine.shape), BF),
                pltpu.VMEM((4, mine.shape[0], quarter), BF),
                pltpu.SemaphoreType.DMA((11,)),
                pltpu.SemaphoreType.DMA((8,)),
            ],
            jnp.stack([z, x, keeps.astype(jnp.int32)]),
            *blocks,
            *weights,
        )

        def summed(terms):
            total = terms[0].astype(F32)
            for dx in (2, 1, 3):
                total = total + shifted(terms[dx], "x", dx).astype(F32)
            return total

        hidden_first = activated(summed(parts[:4]), CROWS)
        hidden_second = activated(summed(parts[4:]), units)
        act_send, _ = lax.optimization_barrier((act_send, incoming_rows))
        outgoing = mm(act_send, hidden_second).astype(BF).reshape(32, CAPACITY, quarter)

    with jax.named_scope("rows"):
        moved = mm(row_place, incoming_rows.reshape(-1, 3 * feats))

        def averaged(first, second):
            return ((first.astype(F32) + second) * 0.5).astype(BF)

        merged = (
            averaged(gate_first, moved[:, :feats]),
            averaged(up_first, moved[:, feats : 2 * feats]),
            averaged(down_first, moved[:, 2 * feats :]),
        )

    with jax.named_scope("window"):
        window = lax.ppermute(hidden_first, AXES, window_perm())
        other = swapped(window, "y_lo")
        both = jnp.concatenate(
            [jnp.where(first_row, window, other), jnp.where(first_row, other, window)], axis=0
        )
        both, _ = lax.optimization_barrier((both, outgoing))
        windows = ring(both, "z", 224)

    with jax.named_scope("matched"):
        incoming = lax.all_to_all(
            outgoing, ("y_lo", "z", "y_hi"), split_axis=0, concat_axis=0, tiled=True
        )
        act_place, merged, _ = lax.optimization_barrier((act_place, merged, windows[2]))
        chosen = mm(act_place, incoming.reshape(-1, quarter)).astype(BF)
        seconds = [*ring(chosen, "x", 224), *ring(swapped(chosen, "y_hi"), "x", 224)]

    with jax.named_scope("correlation"):
        own, theirs = on_device(
            products_kernel,
            [jax.ShapeDtypeStruct((units, 4 * CROWS), F32)] * 2,
            [
                pltpu.VMEM((4, 4 * CROWS, quarter), BF),
                pltpu.VMEM((4, 2, units, quarter), BF),
                pltpu.VMEM((2, units, 4 * CROWS), F32),
                pltpu.SemaphoreType.DMA((19,)),
                pltpu.SemaphoreType.DMA((2,)),
            ],
            jnp.stack([z, x, yh ^ c]),
            *windows,
            *seconds,
        )
        correlation = ((own + swapped(theirs, "core")) * (1.0 / math.sqrt(32 * rows))).T
    return (*merged, correlation)


def solution(mesh):
    split = Mesh(mesh.devices.reshape(2, 8, 2, 2, 4), AXES)
    placed = (*(P(DP, MP),) * 7, P())
    return jax.shard_map(
        local,
        mesh=split,
        in_specs=placed,
        out_specs=(P(DP, MP), P(DP, MP), P(DP, MP), P(MP, DP)),
        check_vma=False,
    )
```

```python
import functools
import math

import jax
import jax.numpy as jnp
from jax import lax
from jax.experimental import pallas as pl
from jax.experimental.pallas import tpu as pltpu
from jax.sharding import Mesh
from jax.sharding import PartitionSpec as P

D = 5120
CROWS = 216
CAPACITY = 16
AXES = ("y_lo", "z", "core", "y_hi", "x")
DP = ("y_lo", "z", "core")
MP = ("y_hi", "x")
CHIPS = ("y_lo", "z")
BF = jnp.bfloat16
F32 = jnp.float32


def shifted(x, axis, k):
    n = lax.axis_size(axis)
    return lax.ppermute(x, axis, [(i, (i + k) % n) for i in range(n)])


def swapped(x, axis):
    return lax.ppermute(x, axis, [(0, 1), (1, 0)])


def ring(block, axis, cut):
    n = lax.axis_size(axis)
    up = down = block
    ups, downs = [], []
    for _ in range(1, n // 2):
        up, down = lax.optimization_barrier((shifted(up, axis, 1), shifted(down, axis, -1)))
        ups.append(up)
        downs.append(down)
    up, down = lax.optimization_barrier((up[:cut], down[cut:]))
    far = [shifted(up, axis, 1), shifted(down, axis, -1)]
    return [block, *downs, *far, *ups[::-1]]


def on_some(x, axes, pairs):
    flat = [(2 * a + b, 2 * c + d) for (a, b), (c, d) in pairs]
    return lax.ppermute(x, axes, flat)


def window_perm():
    def flat(yl, z, c, yh, x):
        return (((yl * 8 + z) * 2 + c) * 2 + yh) * 4 + x

    return [
        (flat(yl, z, c, yh, x), flat(yh, x * 2 + z % 2, c, yl, z // 2))
        for yl in range(2)
        for z in range(8)
        for c in range(2)
        for yh in range(2)
        for x in range(4)
    ]


def one_hot(index, size):
    return (index[:, None] == lax.broadcasted_iota(jnp.int32, (index.shape[0], size), 1)).astype(BF)


def mm(a, b):
    return jnp.dot(a, b, preferred_element_type=F32)


def nt(a, b):
    return lax.dot_general(a, b, (((1,), (1,)), ((), ())), preferred_element_type=F32)


def routes(matching, count, me, capacity):
    groups = matching.reshape(-1, count)
    number = groups.shape[0]
    owned = lax.div(groups, count) == me
    before = lax.broadcasted_iota(jnp.int32, (count, count), 0) < lax.broadcasted_iota(
        jnp.int32, (count, count), 1
    )
    before = before.astype(BF)
    rank = mm(owned.astype(BF), before).astype(jnp.int32)
    slots = jnp.arange(capacity, dtype=jnp.int32)
    picked = owned[:, None, :] & (rank[:, None, :] == slots[None, :, None])
    offsets = lax.rem(groups, count)
    send = jnp.sum(jnp.where(picked, offsets[:, None, :], 0), axis=2).reshape(-1)
    mine = lax.dynamic_slice_in_dim(matching, me * count, count)
    owner = lax.div(mine, count)
    from_block = owner[:, None] == lax.broadcasted_iota(jnp.int32, (count, number), 1)
    arrival = lax.dot_general(
        before, from_block.astype(BF), (((0,), (0,)), ((), ())), preferred_element_type=F32
    )
    arrival = jnp.sum(jnp.where(from_block, arrival, 0.0), axis=1).astype(jnp.int32)
    return one_hot(send, count), owner * capacity + arrival


def ring_pieces(n):
    half = n // 2
    return [(k, False) for k in range(half + 1)] + [(k, k == half) for k in range(half, n)]


def terms_kernel(factor, place_ref, *refs):
    pieces, (mine, near_shared, far_mine, far_shared) = refs[:9], refs[9:13]
    outs, (held, weights, made, arrived, left) = refs[13:21], refs[21:]
    z, x, keeps = place_ref[0], place_ref[1], place_ref[2]
    block_rows = held.shape[1] // 2
    feats = weights.shape[2]
    split = outs[4].shape[0]
    groups = (slice(split, weights.shape[1]), slice(0, split))

    def weights_of(group):
        waits = []
        for slot, (own, shared) in enumerate(((mine, near_shared), (far_mine, far_shared))):
            place, sem = weights.at[slot, groups[group]], arrived.at[9 + 2 * group + slot]
            from_own = pltpu.make_async_copy(own.at[groups[group]], place, sem)
            from_shared = pltpu.make_async_copy(shared.at[groups[group]], place, sem)
            pl.when(keeps == 1)(from_own.start)
            pl.when(keeps == 0)(from_shared.start)
            waits.append(from_own)
        return waits

    first_weights = weights_of(0)
    copies = []
    for (k, second), piece in zip(ring_pieces(8), pieces):
        at = lax.rem(z + k, 8)
        count = piece.shape[0]
        row = lax.rem(at, 2) * block_rows + (block_rows - count if second else 0)
        place = held.at[lax.div(at, 2), pl.ds(pl.multiple_of(row, 16), count)]
        copies.append(pltpu.make_async_copy(piece, place, arrived.at[len(copies)]))
        copies[-1].start()
    second_weights = weights_of(1)
    for copy in copies:
        copy.wait()
    sent = []
    for group, waits in enumerate((first_weights, second_weights)):
        for copy in waits:
            copy.wait()
        rows = groups[group]
        for dx in (2, 1, 3, 0):
            block = held[lax.rem(x + dx, 4)]
            total = nt(weights[0, rows], block[:, :feats]) + nt(weights[1, rows], block[:, feats:])
            made[dx, rows] = (total * factor).astype(BF)
            out = outs[4 * group + dx]
            sent.append(pltpu.make_async_copy(made.at[dx, rows], out, left.at[4 * group + dx]))
            sent[-1].start()
    for copy in sent:
        copy.wait()


def product_kernel(slot, place_ref, *refs):
    windows, near, far, out = refs[:9], refs[9:13], refs[13:17], refs[17]
    held_window, held_second, arrived = refs[18:]
    z, x, flip = place_ref[0], place_ref[1], place_ref[2]
    height = held_window.shape[0] // 2
    width = windows[0].shape[1]
    copies = []

    def lanes(at):
        return pl.ds(pl.multiple_of(at * width, width), width)

    for (k, second), piece in zip(ring_pieces(8), windows):
        at = lax.rem(z + k, 8)
        count = piece.shape[0]
        row = lax.rem(at, 2) * height + (height - count if second else 0)
        place = held_window.at[pl.ds(pl.multiple_of(row, 16), count), lanes(lax.div(at, 2))]
        copies.append(pltpu.make_async_copy(piece, place, arrived.at[len(copies)]))
        copies[-1].start()
    for k in range(4):
        place, sem = held_second.at[:, lanes(lax.rem(x + k, 4))], arrived.at[9 + k]
        from_near = pltpu.make_async_copy(near[k], place, sem)
        from_far = pltpu.make_async_copy(far[k], place, sem)
        pl.when(flip == slot)(from_near.start)
        pl.when(flip != slot)(from_far.start)
        copies.append(from_near)
    for copy in copies:
        copy.wait()
    out[...] = nt(held_second[...], held_window[...])


def on_device(kernel, shapes, out_space, scratch, place, *arrays):
    in_hbm = pl.BlockSpec(memory_space=pl.ANY)
    return pl.pallas_call(
        kernel,
        out_shape=shapes,
        in_specs=[pl.BlockSpec(memory_space=pltpu.SMEM)] + [in_hbm] * len(arrays),
        out_specs=[pl.BlockSpec(memory_space=out_space)] * len(shapes),
        scratch_shapes=scratch,
        compiler_params=pltpu.CompilerParams(vmem_limit_bytes=24 << 20),
    )(place, *arrays)


def activated(pre, count):
    return (jax.nn.silu(pre[:count]) * pre[count:]).astype(BF)


def local(tokens, gate_first, up_first, down_first, gate_second, up_second, down_second, matching):
    units, feats = gate_first.shape
    yl, z, c, yh, x = (lax.axis_index(a) for a in AXES)
    chip = lax.axis_index(CHIPS)
    rows = tokens.shape[0]
    quarter = 4 * rows
    factor = 1.0 / math.sqrt(D)

    with jax.named_scope("tokens"):
        near_other = swapped(tokens, "y_lo")
        far_own = swapped(tokens, "y_hi")
        far_other = lax.ppermute(tokens, ("y_lo", "y_hi"), [(i, 3 - i) for i in range(4)])
        first_row = yl == 0
        pair = jnp.concatenate(
            [
                jnp.concatenate(
                    [jnp.where(first_row, own, other), jnp.where(first_row, other, own)], axis=0
                )
                for own, other in ((tokens, near_other), (far_own, far_other))
            ],
            axis=1,
        )

    with jax.named_scope("weights"):
        mine = jnp.concatenate([gate_second, up_second, gate_first[:CROWS], up_first[:CROWS]], axis=0)

    pair, mine, gate_second, up_second, down_second, matching = lax.optimization_barrier(
        (pair, mine, gate_second, up_second, down_second, matching)
    )

    with jax.named_scope("tokens"):
        blocks = ring(pair, "z", rows)

    with jax.named_scope("weights"):
        keeps = c == yh
        pairs_far = [((0, 1), (0, 0)), ((1, 0), (1, 1))]
        pairs_core = [((0, 0), (1, 0)), ((1, 1), (0, 1))]
        near_shared = on_some(mine, ("core", "y_hi"), pairs_core)
        far = on_some(mine, ("core", "y_hi"), pairs_far)
        far, _ = lax.optimization_barrier((far, blocks[3]))
        far_shared = on_some(far, ("core", "y_hi"), pairs_core)
        weights = (mine, near_shared, far, far_shared)

    with jax.named_scope("routing"):
        row_send, row_land = routes(matching, units, 2 * chip + c, CAPACITY)
        act_send, act_land = routes(matching, units, 2 * chip + yh, CAPACITY)
        row_place = one_hot(row_land, 32 * CAPACITY)
        act_place = one_hot(act_land, 32 * CAPACITY)

    with jax.named_scope("rows"):
        row_send, _ = lax.optimization_barrier((row_send, blocks[1]))
        second_rows = jnp.concatenate([gate_second, up_second, down_second], axis=1)
        outgoing_rows = mm(row_send, second_rows).astype(BF).reshape(32, CAPACITY, 3 * feats)
        outgoing_rows, _ = lax.optimization_barrier((outgoing_rows, blocks[4:6]))
        incoming_rows = lax.all_to_all(outgoing_rows, DP, split_axis=0, concat_axis=0, tiled=True)

    with jax.named_scope("sums"):
        first_parts = [jax.ShapeDtypeStruct((2 * CROWS, quarter), BF)] * 4
        second_parts = [jax.ShapeDtypeStruct((2 * units, quarter), BF)] * 4
        parts = on_device(
            functools.partial(terms_kernel, factor),
            [*first_parts, *second_parts],
            pl.ANY,
            [
                pltpu.VMEM((4, 4 * rows, 2 * feats), BF),
                pltpu.VMEM((2, *mine.shape), BF),
                pltpu.VMEM((4, mine.shape[0], quarter), BF),
                pltpu.SemaphoreType.DMA((13,)),
                pltpu.SemaphoreType.DMA((8,)),
            ],
            jnp.stack([z, x, keeps.astype(jnp.int32)]),
            *blocks,
            *weights,
        )

        def summed(terms):
            total = terms[0].astype(F32)
            for dx in (2, 1, 3):
                total = total + shifted(terms[dx], "x", dx).astype(F32)
            return total

        hidden_first = activated(summed(parts[:4]), CROWS)
        hidden_second = activated(summed(parts[4:]), units)
        act_send, _ = lax.optimization_barrier((act_send, incoming_rows))
        outgoing = mm(act_send, hidden_second).astype(BF).reshape(32, CAPACITY, quarter)

    with jax.named_scope("rows"):
        moved = mm(row_place, incoming_rows.reshape(-1, 3 * feats))

        def averaged(first, second):
            return ((first.astype(F32) + second) * 0.5).astype(BF)

        merged = (
            averaged(gate_first, moved[:, :feats]),
            averaged(up_first, moved[:, feats : 2 * feats]),
            averaged(down_first, moved[:, 2 * feats :]),
        )

    with jax.named_scope("window"):
        window = lax.ppermute(hidden_first, AXES, window_perm())
        other = swapped(window, "y_lo")
        both = jnp.concatenate(
            [jnp.where(first_row, window, other), jnp.where(first_row, other, window)], axis=0
        )
        both, _ = lax.optimization_barrier((both, outgoing))
        windows = ring(both, "z", 224)

    with jax.named_scope("matched"):
        incoming = lax.all_to_all(
            outgoing, ("y_lo", "z", "y_hi"), split_axis=0, concat_axis=0, tiled=True
        )
        act_place, _ = lax.optimization_barrier((act_place, windows[1]))
        chosen = mm(act_place, incoming.reshape(-1, quarter)).astype(BF)
        other = swapped(chosen, "y_hi")
        near = [chosen, *(shifted(chosen, "x", -k) for k in range(1, 4))]
        other, merged = lax.optimization_barrier((other, merged))
        far = [other, *(shifted(other, "x", -k) for k in range(1, 4))]

    with jax.named_scope("correlation"):
        place = jnp.stack([z, x, yh ^ c])
        own, theirs = (
            on_device(
                functools.partial(product_kernel, slot),
                [jax.ShapeDtypeStruct((units, 4 * CROWS), F32)],
                pltpu.VMEM,
                [
                    pltpu.VMEM((4 * CROWS, 4 * quarter), BF),
                    pltpu.VMEM((units, 4 * quarter), BF),
                    pltpu.SemaphoreType.DMA((13,)),
                ],
                place,
                *windows,
                *near,
                *far,
            )[0]
            for slot in range(2)
        )
        correlation = ((own + swapped(theirs, "core")) * (1.0 / math.sqrt(32 * rows))).T
    return (*merged, correlation)


def solution(mesh):
    split = Mesh(mesh.devices.reshape(2, 8, 2, 2, 4), AXES)
    placed = (*(P(DP, MP),) * 7, P())
    return jax.shard_map(
        local,
        mesh=split,
        in_specs=placed,
        out_specs=(P(DP, MP), P(DP, MP), P(DP, MP), P(MP, DP)),
        check_vma=False,
    )
```

```python
import functools
import math

import jax
import jax.numpy as jnp
from jax import lax
from jax.experimental import pallas as pl
from jax.experimental.pallas import tpu as pltpu
from jax.sharding import Mesh
from jax.sharding import PartitionSpec as P

D = 5120
CROWS = 216
CAPACITY = 16
AXES = ("y_lo", "z", "core", "y_hi", "x")
DP = ("y_lo", "z", "core")
MP = ("y_hi", "x")
CHIPS = ("y_lo", "z")
BF = jnp.bfloat16
F32 = jnp.float32


def shifted(x, axis, k):
    n = lax.axis_size(axis)
    return lax.ppermute(x, axis, [(i, (i + k) % n) for i in range(n)])


def swapped(x, axis):
    return lax.ppermute(x, axis, [(0, 1), (1, 0)])


def ring(block, axis, cut):
    n = lax.axis_size(axis)
    up = down = block
    ups, downs = [], []
    for _ in range(1, n // 2):
        up, down = lax.optimization_barrier((shifted(up, axis, 1), shifted(down, axis, -1)))
        ups.append(up)
        downs.append(down)
    up, down = lax.optimization_barrier((up[:cut], down[cut:]))
    far = [shifted(up, axis, 1), shifted(down, axis, -1)]
    return [block, *downs, *far, *ups[::-1]]


def on_some(x, axes, pairs):
    flat = [(2 * a + b, 2 * c + d) for (a, b), (c, d) in pairs]
    return lax.ppermute(x, axes, flat)


def window_perm():
    def flat(yl, z, c, yh, x):
        return (((yl * 8 + z) * 2 + c) * 2 + yh) * 4 + x

    return [
        (flat(yl, z, c, yh, x), flat(yh, x * 2 + z % 2, c, yl, z // 2))
        for yl in range(2)
        for z in range(8)
        for c in range(2)
        for yh in range(2)
        for x in range(4)
    ]


def one_hot(index, size):
    return (index[:, None] == lax.broadcasted_iota(jnp.int32, (index.shape[0], size), 1)).astype(BF)


def mm(a, b):
    return jnp.dot(a, b, preferred_element_type=F32)


def nt(a, b):
    return lax.dot_general(a, b, (((1,), (1,)), ((), ())), preferred_element_type=F32)


def earlier(count):
    return (
        lax.broadcasted_iota(jnp.int32, (count, count), 0)
        < lax.broadcasted_iota(jnp.int32, (count, count), 1)
    ).astype(BF)


def send_matrix(matching, count, me, capacity):
    groups = matching.reshape(-1, count)
    owned = lax.div(groups, count) == me
    rank = mm(owned.astype(BF), earlier(count)).astype(jnp.int32)
    slots = jnp.arange(capacity, dtype=jnp.int32)
    picked = owned[:, None, :] & (rank[:, None, :] == slots[None, :, None])
    offsets = lax.rem(groups, count)
    send = jnp.sum(jnp.where(picked, offsets[:, None, :], 0), axis=2).reshape(-1)
    return one_hot(send, count)


def place_matrix(matching, count, me, capacity):
    number = matching.shape[0] // count
    mine = lax.dynamic_slice_in_dim(matching, me * count, count)
    owner = lax.div(mine, count)
    from_block = owner[:, None] == lax.broadcasted_iota(jnp.int32, (count, number), 1)
    arrival = lax.dot_general(
        earlier(count),
        from_block.astype(BF),
        (((0,), (0,)), ((), ())),
        preferred_element_type=F32,
    )
    arrival = jnp.sum(jnp.where(from_block, arrival, 0.0), axis=1).astype(jnp.int32)
    return one_hot(owner * capacity + arrival, number * capacity)


def ring_pieces(n):
    half = n // 2
    return [(k, False) for k in range(half + 1)] + [(k, k == half) for k in range(half, n)]


def terms_kernel(factor, place_ref, *refs):
    pieces, (mine, first_got, second_got) = refs[:9], refs[9:12]
    outs, (held, weights, made, arrived, left) = refs[12:20], refs[20:]
    z, x, keeps = place_ref[0], place_ref[1], place_ref[2]
    block_rows = held.shape[1] // 2
    feats = mine.shape[1]
    split = outs[4].shape[0]
    groups = (slice(split, weights.shape[0]), slice(0, split))

    def weights_of(group):
        waits = []
        for slot, (own, shared) in enumerate(((mine, first_got), (first_got, second_got))):
            lanes = slice(slot * feats, (slot + 1) * feats)
            place, sem = weights.at[groups[group], lanes], arrived.at[9 + 2 * group + slot]
            from_own = pltpu.make_async_copy(own.at[groups[group]], place, sem)
            from_shared = pltpu.make_async_copy(shared.at[groups[group]], place, sem)
            pl.when(keeps == 1)(from_own.start)
            pl.when(keeps == 0)(from_shared.start)
            waits.append(from_own)
        return waits

    first_weights = weights_of(0)
    copies = []
    for (k, second), piece in zip(ring_pieces(8), pieces):
        at = lax.rem(z + k, 8)
        count = piece.shape[0]
        row = lax.rem(at, 2) * block_rows + (block_rows - count if second else 0)
        place = held.at[lax.div(at, 2), pl.ds(pl.multiple_of(row, 16), count)]
        copies.append(pltpu.make_async_copy(piece, place, arrived.at[len(copies)]))
        copies[-1].start()
    second_weights = weights_of(1)
    for copy in copies:
        copy.wait()
    sent = []
    for group, waits in enumerate((first_weights, second_weights)):
        for copy in waits:
            copy.wait()
        rows = groups[group]
        for dx in (2, 1, 3, 0):
            block = held[lax.rem(x + dx, 4)]
            made[dx, rows] = (nt(weights[rows, :], block) * factor).astype(BF)
            out = outs[4 * group + dx]
            sent.append(pltpu.make_async_copy(made.at[dx, rows], out, left.at[4 * group + dx]))
            sent[-1].start()
    for copy in sent:
        copy.wait()


def product_kernel(slot, place_ref, *refs):
    windows, near, far, out = refs[:9], refs[9:13], refs[13:17], refs[17]
    held_window, held_second, arrived = refs[18:]
    z, x, flip = place_ref[0], place_ref[1], place_ref[2]
    height = held_window.shape[0] // 2
    width = windows[0].shape[1]
    copies = []

    def lanes(at):
        return pl.ds(pl.multiple_of(at * width, width), width)

    for (k, second), piece in zip(ring_pieces(8), windows):
        at = lax.rem(z + k, 8)
        count = piece.shape[0]
        row = lax.rem(at, 2) * height + (height - count if second else 0)
        place = held_window.at[pl.ds(pl.multiple_of(row, 16), count), lanes(lax.div(at, 2))]
        copies.append(pltpu.make_async_copy(piece, place, arrived.at[len(copies)]))
        copies[-1].start()
    for k in range(4):
        place, sem = held_second.at[:, lanes(lax.rem(x + k, 4))], arrived.at[9 + k]
        from_near = pltpu.make_async_copy(near[k], place, sem)
        from_far = pltpu.make_async_copy(far[k], place, sem)
        pl.when(flip == slot)(from_near.start)
        pl.when(flip != slot)(from_far.start)
        copies.append(from_near)
    for copy in copies:
        copy.wait()
    out[...] = nt(held_second[...], held_window[...])


def on_device(kernel, shapes, out_space, scratch, place, *arrays):
    in_hbm = pl.BlockSpec(memory_space=pl.ANY)
    return pl.pallas_call(
        kernel,
        out_shape=shapes,
        in_specs=[pl.BlockSpec(memory_space=pltpu.SMEM)] + [in_hbm] * len(arrays),
        out_specs=[pl.BlockSpec(memory_space=out_space)] * len(shapes),
        scratch_shapes=scratch,
        compiler_params=pltpu.CompilerParams(vmem_limit_bytes=24 << 20),
    )(place, *arrays)


def activated(pre, count):
    return (jax.nn.silu(pre[:count]) * pre[count:]).astype(BF)


def local(tokens, gate_first, up_first, down_first, gate_second, up_second, down_second, matching):
    units, feats = gate_first.shape
    yl, z, c, yh, x = (lax.axis_index(a) for a in AXES)
    chip = lax.axis_index(CHIPS)
    rows = tokens.shape[0]
    quarter = 4 * rows
    factor = 1.0 / math.sqrt(D)

    with jax.named_scope("tokens"):
        near_other = swapped(tokens, "y_lo")
        far_own = swapped(tokens, "y_hi")
        far_other = lax.ppermute(tokens, ("y_lo", "y_hi"), [(i, 3 - i) for i in range(4)])
        first_row = yl == 0
        pair = jnp.concatenate(
            [
                jnp.concatenate(
                    [jnp.where(first_row, own, other), jnp.where(first_row, other, own)], axis=0
                )
                for own, other in ((tokens, near_other), (far_own, far_other))
            ],
            axis=1,
        )

    with jax.named_scope("weights"):
        mine = jnp.concatenate([gate_second, up_second, gate_first[:CROWS], up_first[:CROWS]], axis=0)

    pair, mine, gate_second, up_second, down_second, matching = lax.optimization_barrier(
        (pair, mine, gate_second, up_second, down_second, matching)
    )

    with jax.named_scope("tokens"):
        blocks = ring(pair, "z", rows)

    with jax.named_scope("weights"):
        keeps = c == yh
        pairs_once = [((0, 1), (0, 0)), ((1, 0), (1, 1)), ((0, 0), (1, 0)), ((1, 1), (0, 1))]
        pairs_core = [((0, 0), (1, 0)), ((1, 1), (0, 1))]
        first_got = on_some(mine, ("core", "y_hi"), pairs_once)
        first_got, _ = lax.optimization_barrier((first_got, blocks[3]))
        second_got = on_some(first_got, ("core", "y_hi"), pairs_core)

    with jax.named_scope("routing"):
        row_send = send_matrix(matching, units, 2 * chip + c, CAPACITY)
        act_send = send_matrix(matching, units, 2 * chip + yh, CAPACITY)
        act_place = place_matrix(matching, units, 2 * chip + yh, CAPACITY)
        row_place = place_matrix(matching, units, 2 * chip + c, CAPACITY)

    with jax.named_scope("rows"):
        row_send, _ = lax.optimization_barrier((row_send, blocks[1]))
        second_rows = jnp.concatenate([gate_second, up_second, down_second], axis=1)
        outgoing_rows = mm(row_send, second_rows).astype(BF).reshape(32, CAPACITY, 3 * feats)
        outgoing_rows, _ = lax.optimization_barrier((outgoing_rows, blocks[4:6]))
        incoming_rows = lax.all_to_all(outgoing_rows, DP, split_axis=0, concat_axis=0, tiled=True)

    with jax.named_scope("sums"):
        first_parts = [jax.ShapeDtypeStruct((2 * CROWS, quarter), BF)] * 4
        second_parts = [jax.ShapeDtypeStruct((2 * units, quarter), BF)] * 4
        parts = on_device(
            functools.partial(terms_kernel, factor),
            [*first_parts, *second_parts],
            pl.ANY,
            [
                pltpu.VMEM((4, 4 * rows, 2 * feats), BF),
                pltpu.VMEM((mine.shape[0], 2 * feats), BF),
                pltpu.VMEM((4, mine.shape[0], quarter), BF),
                pltpu.SemaphoreType.DMA((13,)),
                pltpu.SemaphoreType.DMA((8,)),
            ],
            jnp.stack([z, x, keeps.astype(jnp.int32)]),
            *blocks,
            mine,
            first_got,
            second_got,
        )

        def summed(terms):
            total = terms[0].astype(F32)
            for dx in (2, 1, 3):
                total = total + shifted(terms[dx], "x", dx).astype(F32)
            return total

        hidden_first = activated(summed(parts[:4]), CROWS)
        hidden_second = activated(summed(parts[4:]), units)
        act_send, _ = lax.optimization_barrier((act_send, incoming_rows))
        outgoing = mm(act_send, hidden_second).astype(BF).reshape(32, CAPACITY, quarter)

    with jax.named_scope("rows"):
        moved = mm(row_place, incoming_rows.reshape(-1, 3 * feats))

        def averaged(first, second):
            return ((first.astype(F32) + second) * 0.5).astype(BF)

        merged = (
            averaged(gate_first, moved[:, :feats]),
            averaged(up_first, moved[:, feats : 2 * feats]),
            averaged(down_first, moved[:, 2 * feats :]),
        )

    with jax.named_scope("window"):
        window = lax.ppermute(hidden_first, AXES, window_perm())
        other = swapped(window, "y_lo")
        both = jnp.concatenate(
            [jnp.where(first_row, window, other), jnp.where(first_row, other, window)], axis=0
        )
        both, _ = lax.optimization_barrier((both, outgoing))
        windows = ring(both, "z", 224)

    with jax.named_scope("matched"):
        incoming = lax.all_to_all(
            outgoing, ("y_lo", "z", "y_hi"), split_axis=0, concat_axis=0, tiled=True
        )
        act_place, _ = lax.optimization_barrier((act_place, windows[1]))
        chosen = mm(act_place, incoming.reshape(-1, quarter)).astype(BF)
        other = swapped(chosen, "y_hi")
        near = [chosen, *(shifted(chosen, "x", -k) for k in range(1, 4))]
        other, merged = lax.optimization_barrier((other, merged))
        far = [other, *(shifted(other, "x", -k) for k in range(1, 4))]

    with jax.named_scope("correlation"):
        place = jnp.stack([z, x, yh ^ c])
        own, theirs = (
            on_device(
                functools.partial(product_kernel, slot),
                [jax.ShapeDtypeStruct((units, 4 * CROWS), F32)],
                pltpu.VMEM,
                [
                    pltpu.VMEM((4 * CROWS, 4 * quarter), BF),
                    pltpu.VMEM((units, 4 * quarter), BF),
                    pltpu.SemaphoreType.DMA((13,)),
                ],
                place,
                *windows,
                *near,
                *far,
            )[0]
            for slot in range(2)
        )
        correlation = ((own + swapped(theirs, "core")) * (1.0 / math.sqrt(32 * rows))).T
    return (*merged, correlation)


def solution(mesh):
    split = Mesh(mesh.devices.reshape(2, 8, 2, 2, 4), AXES)
    placed = (*(P(DP, MP),) * 7, P())
    return jax.shard_map(
        local,
        mesh=split,
        in_specs=placed,
        out_specs=(P(DP, MP), P(DP, MP), P(DP, MP), P(MP, DP)),
        check_vma=False,
    )
```

```python
import functools
import math

import jax
import jax.numpy as jnp
from jax import lax
from jax.experimental import pallas as pl
from jax.experimental.pallas import tpu as pltpu
from jax.sharding import Mesh
from jax.sharding import PartitionSpec as P

D = 5120
CROWS = 216
CAPACITY = 16
AXES = ("y_lo", "z", "core", "y_hi", "x")
DP = ("y_lo", "z", "core")
MP = ("y_hi", "x")
CHIPS = ("y_lo", "z")
BF = jnp.bfloat16
F32 = jnp.float32


def shifted(x, axis, k):
    n = lax.axis_size(axis)
    return lax.ppermute(x, axis, [(i, (i + k) % n) for i in range(n)])


def swapped(x, axis):
    return lax.ppermute(x, axis, [(0, 1), (1, 0)])


def ring(block, axis, cut):
    n = lax.axis_size(axis)
    up = down = block
    ups, downs = [], []
    for _ in range(1, n // 2):
        up, down = lax.optimization_barrier((shifted(up, axis, 1), shifted(down, axis, -1)))
        ups.append(up)
        downs.append(down)
    up, down = lax.optimization_barrier((up[:cut], down[cut:]))
    far = [shifted(up, axis, 1), shifted(down, axis, -1)]
    return [block, *downs, *far, *ups[::-1]]


def on_some(x, axes, pairs):
    flat = [(2 * a + b, 2 * c + d) for (a, b), (c, d) in pairs]
    return lax.ppermute(x, axes, flat)


def window_perm():
    def flat(yl, z, c, yh, x):
        return (((yl * 8 + z) * 2 + c) * 2 + yh) * 4 + x

    return [
        (flat(yl, z, c, yh, x), flat(yh, x * 2 + z % 2, c, yl, z // 2))
        for yl in range(2)
        for z in range(8)
        for c in range(2)
        for yh in range(2)
        for x in range(4)
    ]


def one_hot(index, size):
    return (index[:, None] == lax.broadcasted_iota(jnp.int32, (index.shape[0], size), 1)).astype(BF)


def mm(a, b):
    return jnp.dot(a, b, preferred_element_type=F32)


def nt(a, b):
    return lax.dot_general(a, b, (((1,), (1,)), ((), ())), preferred_element_type=F32)


def earlier(count):
    return (
        lax.broadcasted_iota(jnp.int32, (count, count), 0)
        < lax.broadcasted_iota(jnp.int32, (count, count), 1)
    ).astype(BF)


def send_matrix(matching, count, me, capacity):
    groups = matching.reshape(-1, count)
    owned = lax.div(groups, count) == me
    rank = mm(owned.astype(BF), earlier(count)).astype(jnp.int32)
    slots = jnp.arange(capacity, dtype=jnp.int32)
    picked = owned[:, None, :] & (rank[:, None, :] == slots[None, :, None])
    offsets = lax.rem(groups, count)
    send = jnp.sum(jnp.where(picked, offsets[:, None, :], 0), axis=2).reshape(-1)
    return one_hot(send, count)


def place_matrix(matching, count, me, capacity):
    number = matching.shape[0] // count
    mine = lax.dynamic_slice_in_dim(matching, me * count, count)
    owner = lax.div(mine, count)
    from_block = owner[:, None] == lax.broadcasted_iota(jnp.int32, (count, number), 1)
    arrival = lax.dot_general(
        earlier(count),
        from_block.astype(BF),
        (((0,), (0,)), ((), ())),
        preferred_element_type=F32,
    )
    arrival = jnp.sum(jnp.where(from_block, arrival, 0.0), axis=1).astype(jnp.int32)
    return one_hot(owner * capacity + arrival, number * capacity)


def ring_pieces(n):
    half = n // 2
    return [(k, False) for k in range(half + 1)] + [(k, k == half) for k in range(half, n)]


def terms_kernel(factor, place_ref, *refs):
    pieces, (mine, first_got, second_got) = refs[:9], refs[9:12]
    outs, (held, weights, made, arrived, left) = refs[12:20], refs[20:]
    z, x, keeps = place_ref[0], place_ref[1], place_ref[2]
    block_rows = held.shape[1] // 2
    feats = mine.shape[1]
    split = outs[4].shape[0]
    groups = (slice(split, weights.shape[0]), slice(0, split))

    def weights_of(group):
        waits = []
        for slot, (own, shared) in enumerate(((mine, first_got), (first_got, second_got))):
            lanes = slice(slot * feats, (slot + 1) * feats)
            place, sem = weights.at[groups[group], lanes], arrived.at[9 + 2 * group + slot]
            from_own = pltpu.make_async_copy(own.at[groups[group]], place, sem)
            from_shared = pltpu.make_async_copy(shared.at[groups[group]], place, sem)
            pl.when(keeps == 1)(from_own.start)
            pl.when(keeps == 0)(from_shared.start)
            waits.append(from_own)
        return waits

    first_weights = weights_of(0)
    copies = []
    for (k, second), piece in zip(ring_pieces(8), pieces):
        at = lax.rem(z + k, 8)
        count = piece.shape[0]
        row = lax.rem(at, 2) * block_rows + (block_rows - count if second else 0)
        place = held.at[lax.div(at, 2), pl.ds(pl.multiple_of(row, 16), count)]
        copies.append(pltpu.make_async_copy(piece, place, arrived.at[len(copies)]))
        copies[-1].start()
    second_weights = weights_of(1)
    for copy in copies:
        copy.wait()
    sent = []
    for group, waits in enumerate((first_weights, second_weights)):
        for copy in waits:
            copy.wait()
        rows = groups[group]
        for dx in (2, 1, 3, 0):
            block = held[lax.rem(x + dx, 4)]
            made[dx, rows] = (nt(weights[rows, :], block) * factor).astype(BF)
            out = outs[4 * group + dx]
            sent.append(pltpu.make_async_copy(made.at[dx, rows], out, left.at[4 * group + dx]))
            sent[-1].start()
    for copy in sent:
        copy.wait()


def product_kernel(slot, place_ref, *refs):
    windows, near, far, out = refs[:9], refs[9:13], refs[13:17], refs[17]
    held_window, held_second, arrived = refs[18:]
    z, x, flip = place_ref[0], place_ref[1], place_ref[2]
    height = held_window.shape[0] // 2
    width = windows[0].shape[1]
    copies = []

    def lanes(at):
        return pl.ds(pl.multiple_of(at * width, width), width)

    for (k, second), piece in zip(ring_pieces(8), windows):
        at = lax.rem(z + k, 8)
        count = piece.shape[0]
        row = lax.rem(at, 2) * height + (height - count if second else 0)
        place = held_window.at[pl.ds(pl.multiple_of(row, 16), count), lanes(lax.div(at, 2))]
        copies.append(pltpu.make_async_copy(piece, place, arrived.at[len(copies)]))
        copies[-1].start()
    for k in range(4):
        place, sem = held_second.at[:, lanes(lax.rem(x + k, 4))], arrived.at[9 + k]
        from_near = pltpu.make_async_copy(near[k], place, sem)
        from_far = pltpu.make_async_copy(far[k], place, sem)
        pl.when(flip == slot)(from_near.start)
        pl.when(flip != slot)(from_far.start)
        copies.append(from_near)
    for copy in copies:
        copy.wait()
    out[...] = nt(held_second[...], held_window[...])


def on_device(kernel, shapes, out_space, scratch, place, *arrays):
    in_hbm = pl.BlockSpec(memory_space=pl.ANY)
    return pl.pallas_call(
        kernel,
        out_shape=shapes,
        in_specs=[pl.BlockSpec(memory_space=pltpu.SMEM)] + [in_hbm] * len(arrays),
        out_specs=[pl.BlockSpec(memory_space=out_space)] * len(shapes),
        scratch_shapes=scratch,
        compiler_params=pltpu.CompilerParams(vmem_limit_bytes=24 << 20),
    )(place, *arrays)


def activated(pre, count):
    return (jax.nn.silu(pre[:count]) * pre[count:]).astype(BF)


def local(tokens, gate_first, up_first, down_first, gate_second, up_second, down_second, matching):
    units, feats = gate_first.shape
    yl, z, c, yh, x = (lax.axis_index(a) for a in AXES)
    chip = lax.axis_index(CHIPS)
    rows = tokens.shape[0]
    quarter = 4 * rows
    factor = 1.0 / math.sqrt(D)

    with jax.named_scope("tokens"):
        near_other = swapped(tokens, "y_lo")
        far_own = swapped(tokens, "y_hi")
        far_other = lax.ppermute(tokens, ("y_lo", "y_hi"), [(i, 3 - i) for i in range(4)])
        first_row = yl == 0
        pair = jnp.concatenate(
            [
                jnp.concatenate(
                    [jnp.where(first_row, own, other), jnp.where(first_row, other, own)], axis=0
                )
                for own, other in ((tokens, near_other), (far_own, far_other))
            ],
            axis=1,
        )

    with jax.named_scope("weights"):
        mine = jnp.concatenate([gate_second, up_second, gate_first[:CROWS], up_first[:CROWS]], axis=0)

    pair, mine, gate_second, up_second, down_second, matching = lax.optimization_barrier(
        (pair, mine, gate_second, up_second, down_second, matching)
    )

    with jax.named_scope("tokens"):
        blocks = ring(pair, "z", rows)

    with jax.named_scope("weights"):
        keeps = c == yh
        pairs_once = [((0, 1), (0, 0)), ((1, 0), (1, 1)), ((0, 0), (1, 0)), ((1, 1), (0, 1))]
        pairs_core = [((0, 0), (1, 0)), ((1, 1), (0, 1))]
        first_got = on_some(mine, ("core", "y_hi"), pairs_once)
        first_got, _ = lax.optimization_barrier((first_got, blocks[3]))
        second_got = on_some(first_got, ("core", "y_hi"), pairs_core)

    with jax.named_scope("routing"):
        row_send = send_matrix(matching, units, 2 * chip + c, CAPACITY)
        act_send = send_matrix(matching, units, 2 * chip + yh, CAPACITY)
        act_place = place_matrix(matching, units, 2 * chip + yh, CAPACITY)
        row_place = place_matrix(matching, units, 2 * chip + c, CAPACITY)

    with jax.named_scope("rows"):
        row_send, act_send, _ = lax.optimization_barrier((row_send, act_send, blocks[1]))
        second_rows = jnp.concatenate([gate_second, up_second, down_second], axis=1)
        outgoing_rows = mm(row_send, second_rows).astype(BF).reshape(32, CAPACITY, 3 * feats)
        outgoing_rows, _ = lax.optimization_barrier((outgoing_rows, blocks[4:6]))
        incoming_rows = lax.all_to_all(outgoing_rows, DP, split_axis=0, concat_axis=0, tiled=True)

    with jax.named_scope("sums"):
        first_parts = [jax.ShapeDtypeStruct((2 * CROWS, quarter), BF)] * 4
        second_parts = [jax.ShapeDtypeStruct((2 * units, quarter), BF)] * 4
        parts = on_device(
            functools.partial(terms_kernel, factor),
            [*first_parts, *second_parts],
            pl.ANY,
            [
                pltpu.VMEM((4, 4 * rows, 2 * feats), BF),
                pltpu.VMEM((mine.shape[0], 2 * feats), BF),
                pltpu.VMEM((4, mine.shape[0], quarter), BF),
                pltpu.SemaphoreType.DMA((13,)),
                pltpu.SemaphoreType.DMA((8,)),
            ],
            jnp.stack([z, x, keeps.astype(jnp.int32)]),
            *blocks,
            mine,
            first_got,
            second_got,
        )

        def summed(terms):
            total = terms[0].astype(F32)
            for dx in (2, 1, 3):
                total = total + shifted(terms[dx], "x", dx).astype(F32)
            return total

        hidden_first = activated(summed(parts[:4]), CROWS)
        hidden_second = activated(summed(parts[4:]), units)
        act_send, _ = lax.optimization_barrier((act_send, incoming_rows))
        outgoing = mm(act_send, hidden_second).astype(BF).reshape(32, CAPACITY, quarter)

    with jax.named_scope("rows"):
        moved = mm(row_place, incoming_rows.reshape(-1, 3 * feats))

        def averaged(first, second):
            return ((first.astype(F32) + second) * 0.5).astype(BF)

        merged = (
            averaged(gate_first, moved[:, :feats]),
            averaged(up_first, moved[:, feats : 2 * feats]),
            averaged(down_first, moved[:, 2 * feats :]),
        )

    with jax.named_scope("window"):
        window = lax.ppermute(hidden_first, AXES, window_perm())
        other = swapped(window, "y_lo")
        both = jnp.concatenate(
            [jnp.where(first_row, window, other), jnp.where(first_row, other, window)], axis=0
        )
        both, _ = lax.optimization_barrier((both, outgoing))
        windows = ring(both, "z", 224)

    with jax.named_scope("matched"):
        incoming = lax.all_to_all(
            outgoing, ("y_lo", "z", "y_hi"), split_axis=0, concat_axis=0, tiled=True
        )
        act_place, merged, _ = lax.optimization_barrier((act_place, merged, windows[1]))
        chosen = mm(act_place, incoming.reshape(-1, quarter)).astype(BF)
        other = swapped(chosen, "y_hi")
        near = [chosen, *(shifted(chosen, "x", -k) for k in range(1, 4))]
        far = [other, *(shifted(other, "x", -k) for k in range(1, 4))]

    with jax.named_scope("correlation"):
        place = jnp.stack([z, x, yh ^ c])
        own, theirs = (
            on_device(
                functools.partial(product_kernel, slot),
                [jax.ShapeDtypeStruct((units, 4 * CROWS), F32)],
                pltpu.VMEM,
                [
                    pltpu.VMEM((4 * CROWS, 4 * quarter), BF),
                    pltpu.VMEM((units, 4 * quarter), BF),
                    pltpu.SemaphoreType.DMA((13,)),
                ],
                place,
                *windows,
                *near,
                *far,
            )[0]
            for slot in range(2)
        )
        correlation = ((own + swapped(theirs, "core")) * (1.0 / math.sqrt(32 * rows))).T
    return (*merged, correlation)


def solution(mesh):
    split = Mesh(mesh.devices.reshape(2, 8, 2, 2, 4), AXES)
    placed = (*(P(DP, MP),) * 7, P())
    return jax.shard_map(
        local,
        mesh=split,
        in_specs=placed,
        out_specs=(P(DP, MP), P(DP, MP), P(DP, MP), P(MP, DP)),
        check_vma=False,
    )
```

```python
import functools
import math

import jax
import jax.numpy as jnp
from jax import lax
from jax.experimental import pallas as pl
from jax.experimental.pallas import tpu as pltpu
from jax.sharding import Mesh
from jax.sharding import PartitionSpec as P

D = 5120
CROWS = 216
CAPACITY = 16
AXES = ("y_lo", "z", "core", "y_hi", "x")
DP = ("y_lo", "z", "core")
MP = ("y_hi", "x")
CHIPS = ("y_lo", "z")
BF = jnp.bfloat16
F32 = jnp.float32


def shifted(x, axis, k):
    n = lax.axis_size(axis)
    return lax.ppermute(x, axis, [(i, (i + k) % n) for i in range(n)])


def swapped(x, axis):
    return lax.ppermute(x, axis, [(0, 1), (1, 0)])


def ring(block, axis, cut):
    n = lax.axis_size(axis)
    up = down = block
    ups, downs = [], []
    for _ in range(1, n // 2):
        up, down = lax.optimization_barrier((shifted(up, axis, 1), shifted(down, axis, -1)))
        ups.append(up)
        downs.append(down)
    up, down = lax.optimization_barrier((up[:cut], down[cut:]))
    far = [shifted(up, axis, 1), shifted(down, axis, -1)]
    return [block, *downs, *far, *ups[::-1]]


def on_some(x, axes, pairs):
    flat = [(2 * a + b, 2 * c + d) for (a, b), (c, d) in pairs]
    return lax.ppermute(x, axes, flat)


def window_perm():
    def flat(yl, z, c, yh, x):
        return (((yl * 8 + z) * 2 + c) * 2 + yh) * 4 + x

    return [
        (flat(yl, z, c, yh, x), flat(yh, x * 2 + z % 2, c, yl, z // 2))
        for yl in range(2)
        for z in range(8)
        for c in range(2)
        for yh in range(2)
        for x in range(4)
    ]


def one_hot(index, size):
    return (index[:, None] == lax.broadcasted_iota(jnp.int32, (index.shape[0], size), 1)).astype(BF)


def mm(a, b):
    return jnp.dot(a, b, preferred_element_type=F32)


def nt(a, b):
    return lax.dot_general(a, b, (((1,), (1,)), ((), ())), preferred_element_type=F32)


def earlier(count):
    return (
        lax.broadcasted_iota(jnp.int32, (count, count), 0)
        < lax.broadcasted_iota(jnp.int32, (count, count), 1)
    ).astype(BF)


def send_matrix(matching, count, me, capacity):
    groups = matching.reshape(-1, count)
    owned = lax.div(groups, count) == me
    rank = mm(owned.astype(BF), earlier(count)).astype(jnp.int32)
    slots = jnp.arange(capacity, dtype=jnp.int32)
    picked = owned[:, None, :] & (rank[:, None, :] == slots[None, :, None])
    offsets = lax.rem(groups, count)
    send = jnp.sum(jnp.where(picked, offsets[:, None, :], 0), axis=2).reshape(-1)
    return one_hot(send, count)


def place_matrix(matching, count, me, capacity):
    number = matching.shape[0] // count
    mine = lax.dynamic_slice_in_dim(matching, me * count, count)
    owner = lax.div(mine, count)
    from_block = owner[:, None] == lax.broadcasted_iota(jnp.int32, (count, number), 1)
    arrival = lax.dot_general(
        earlier(count),
        from_block.astype(BF),
        (((0,), (0,)), ((), ())),
        preferred_element_type=F32,
    )
    arrival = jnp.sum(jnp.where(from_block, arrival, 0.0), axis=1).astype(jnp.int32)
    return one_hot(owner * capacity + arrival, number * capacity)


def ring_pieces(n):
    half = n // 2
    return [(k, False) for k in range(half + 1)] + [(k, k == half) for k in range(half, n)]


def terms_kernel(factor, place_ref, *refs):
    pieces, (second_got, mine, first_got) = refs[:9], refs[9:12]
    outs, (held, weights, made, arrived, left) = refs[12:20], refs[20:]
    z, x, keeps = place_ref[0], place_ref[1], place_ref[2]
    block_rows = held.shape[1] // 2
    feats = mine.shape[1]
    split = outs[4].shape[0]
    groups = (slice(split, weights.shape[0]), slice(0, split))

    def weights_of(group):
        waits = []
        for slot, (own, shared) in enumerate(((mine, first_got), (first_got, second_got))):
            lanes = slice(slot * feats, (slot + 1) * feats)
            place, sem = weights.at[groups[group], lanes], arrived.at[9 + 2 * group + slot]
            from_own = pltpu.make_async_copy(own.at[groups[group]], place, sem)
            from_shared = pltpu.make_async_copy(shared.at[groups[group]], place, sem)
            pl.when(keeps == 1)(from_own.start)
            pl.when(keeps == 0)(from_shared.start)
            waits.append(from_own)
        return waits

    first_weights = weights_of(0)
    copies = []
    for (k, second), piece in zip(ring_pieces(8), pieces):
        at = lax.rem(z + k, 8)
        count = piece.shape[0]
        row = lax.rem(at, 2) * block_rows + (block_rows - count if second else 0)
        place = held.at[lax.div(at, 2), pl.ds(pl.multiple_of(row, 16), count)]
        copies.append(pltpu.make_async_copy(piece, place, arrived.at[len(copies)]))
        copies[-1].start()
    second_weights = weights_of(1)
    for copy in copies:
        copy.wait()
    sent = []
    for group, waits in enumerate((first_weights, second_weights)):
        for copy in waits:
            copy.wait()
        rows = groups[group]
        for dx in (2, 1, 3, 0):
            block = held[lax.rem(x + dx, 4)]
            made[dx, rows] = (nt(weights[rows, :], block) * factor).astype(BF)
            out = outs[4 * group + dx]
            sent.append(pltpu.make_async_copy(made.at[dx, rows], out, left.at[4 * group + dx]))
            sent[-1].start()
    for copy in sent:
        copy.wait()


def product_kernel(slot, place_ref, *refs):
    windows, near, far, out = refs[:9], refs[9:13], refs[13:17], refs[17]
    held_window, held_second, arrived = refs[18:]
    z, x, flip = place_ref[0], place_ref[1], place_ref[2]
    height = held_window.shape[0] // 2
    width = windows[0].shape[1]
    copies = []

    def lanes(at):
        return pl.ds(pl.multiple_of(at * width, width), width)

    for (k, second), piece in zip(ring_pieces(8), windows):
        at = lax.rem(z + k, 8)
        count = piece.shape[0]
        row = lax.rem(at, 2) * height + (height - count if second else 0)
        place = held_window.at[pl.ds(pl.multiple_of(row, 16), count), lanes(lax.div(at, 2))]
        copies.append(pltpu.make_async_copy(piece, place, arrived.at[len(copies)]))
        copies[-1].start()
    for k in range(4):
        place, sem = held_second.at[:, lanes(lax.rem(x + k, 4))], arrived.at[9 + k]
        from_near = pltpu.make_async_copy(near[k], place, sem)
        from_far = pltpu.make_async_copy(far[k], place, sem)
        pl.when(flip == slot)(from_near.start)
        pl.when(flip != slot)(from_far.start)
        copies.append(from_near)
    for copy in copies:
        copy.wait()
    out[...] = nt(held_second[...], held_window[...])


def on_device(kernel, shapes, out_space, scratch, place, *arrays, near=0):
    in_hbm = pl.BlockSpec(memory_space=pl.ANY)
    return pl.pallas_call(
        kernel,
        out_shape=shapes,
        in_specs=[pl.BlockSpec(memory_space=pltpu.SMEM)] + [in_hbm] * len(arrays),
        out_specs=[pl.BlockSpec(memory_space=out_space)] * len(shapes),
        scratch_shapes=scratch,
        compiler_params=pltpu.CompilerParams(vmem_limit_bytes=24 << 20),
    )(place, *arrays)


def activated(pre, count):
    return (jax.nn.silu(pre[:count]) * pre[count:]).astype(BF)


def local(tokens, gate_first, up_first, down_first, gate_second, up_second, down_second, matching):
    units, feats = gate_first.shape
    yl, z, c, yh, x = (lax.axis_index(a) for a in AXES)
    chip = lax.axis_index(CHIPS)
    rows = tokens.shape[0]
    quarter = 4 * rows
    factor = 1.0 / math.sqrt(D)

    with jax.named_scope("tokens"):
        near_other = swapped(tokens, "y_lo")
        far_own = swapped(tokens, "y_hi")
        far_other = lax.ppermute(tokens, ("y_lo", "y_hi"), [(i, 3 - i) for i in range(4)])
        first_row = yl == 0
        pair = jnp.concatenate(
            [
                jnp.concatenate(
                    [jnp.where(first_row, own, other), jnp.where(first_row, other, own)], axis=0
                )
                for own, other in ((tokens, near_other), (far_own, far_other))
            ],
            axis=1,
        )

    with jax.named_scope("weights"):
        mine = jnp.concatenate([gate_second, up_second, gate_first[:CROWS], up_first[:CROWS]], axis=0)

    pair, mine, gate_second, up_second, down_second, matching = lax.optimization_barrier(
        (pair, mine, gate_second, up_second, down_second, matching)
    )

    with jax.named_scope("tokens"):
        blocks = ring(pair, "z", rows)

    with jax.named_scope("weights"):
        keeps = c == yh
        pairs_once = [((0, 1), (0, 0)), ((1, 0), (1, 1)), ((0, 0), (1, 0)), ((1, 1), (0, 1))]
        pairs_core = [((0, 0), (1, 0)), ((1, 1), (0, 1))]
        first_got = on_some(mine, ("core", "y_hi"), pairs_once)
        first_got, _ = lax.optimization_barrier((first_got, blocks[3]))
        second_got = on_some(first_got, ("core", "y_hi"), pairs_core)

    with jax.named_scope("routing"):
        row_send = send_matrix(matching, units, 2 * chip + c, CAPACITY)
        act_send = send_matrix(matching, units, 2 * chip + yh, CAPACITY)
        act_place = place_matrix(matching, units, 2 * chip + yh, CAPACITY)
        row_place = place_matrix(matching, units, 2 * chip + c, CAPACITY)

    with jax.named_scope("rows"):
        row_send, act_send, _ = lax.optimization_barrier((row_send, act_send, blocks[1]))
        second_rows = jnp.concatenate([gate_second, up_second, down_second], axis=1)
        outgoing_rows = mm(row_send, second_rows).astype(BF).reshape(32, CAPACITY, 3 * feats)
        outgoing_rows, _ = lax.optimization_barrier((outgoing_rows, blocks[4:6]))
        incoming_rows = lax.all_to_all(outgoing_rows, DP, split_axis=0, concat_axis=0, tiled=True)

    with jax.named_scope("sums"):
        first_parts = [jax.ShapeDtypeStruct((2 * CROWS, quarter), BF)] * 4
        second_parts = [jax.ShapeDtypeStruct((2 * units, quarter), BF)] * 4
        parts = on_device(
            functools.partial(terms_kernel, factor),
            [*first_parts, *second_parts],
            pl.ANY,
            [
                pltpu.VMEM((4, 4 * rows, 2 * feats), BF),
                pltpu.VMEM((mine.shape[0], 2 * feats), BF),
                pltpu.VMEM((4, mine.shape[0], quarter), BF),
                pltpu.SemaphoreType.DMA((13,)),
                pltpu.SemaphoreType.DMA((8,)),
            ],
            jnp.stack([z, x, keeps.astype(jnp.int32)]),
            *blocks,
            second_got,
            mine,
            first_got,
            near=2,
        )

        def summed(terms):
            total = terms[0].astype(F32)
            for dx in (2, 1, 3):
                total = total + shifted(terms[dx], "x", dx).astype(F32)
            return total

        hidden_first = activated(summed(parts[:4]), CROWS)
        hidden_second = activated(summed(parts[4:]), units)
        act_send, _ = lax.optimization_barrier((act_send, incoming_rows))
        outgoing = mm(act_send, hidden_second).astype(BF).reshape(32, CAPACITY, quarter)

    with jax.named_scope("rows"):
        moved = mm(row_place, incoming_rows.reshape(-1, 3 * feats))

        def averaged(first, second):
            return ((first.astype(F32) + second) * 0.5).astype(BF)

        merged = (
            averaged(gate_first, moved[:, :feats]),
            averaged(up_first, moved[:, feats : 2 * feats]),
            averaged(down_first, moved[:, 2 * feats :]),
        )

    with jax.named_scope("window"):
        window = lax.ppermute(hidden_first, AXES, window_perm())
        other = swapped(window, "y_lo")
        both = jnp.concatenate(
            [jnp.where(first_row, window, other), jnp.where(first_row, other, window)], axis=0
        )
        both, _ = lax.optimization_barrier((both, outgoing))
        windows = ring(both, "z", 224)

    with jax.named_scope("matched"):
        incoming = lax.all_to_all(
            outgoing, ("y_lo", "z", "y_hi"), split_axis=0, concat_axis=0, tiled=True
        )
        act_place, merged, _ = lax.optimization_barrier((act_place, merged, windows[1]))
        chosen = mm(act_place, incoming.reshape(-1, quarter)).astype(BF)
        other = swapped(chosen, "y_hi")
        near = [chosen, *(shifted(chosen, "x", -k) for k in range(1, 4))]
        far = [other, *(shifted(other, "x", -k) for k in range(1, 4))]

    with jax.named_scope("correlation"):
        place = jnp.stack([z, x, yh ^ c])
        own, theirs = (
            on_device(
                functools.partial(product_kernel, slot),
                [jax.ShapeDtypeStruct((units, 4 * CROWS), F32)],
                pltpu.VMEM,
                [
                    pltpu.VMEM((4 * CROWS, 4 * quarter), BF),
                    pltpu.VMEM((units, 4 * quarter), BF),
                    pltpu.SemaphoreType.DMA((13,)),
                ],
                place,
                *windows,
                *near,
                *far,
            )[0]
            for slot in range(2)
        )
        correlation = ((own + swapped(theirs, "core")) * (1.0 / math.sqrt(32 * rows))).T
    return (*merged, correlation)


def solution(mesh):
    split = Mesh(mesh.devices.reshape(2, 8, 2, 2, 4), AXES)
    placed = (*(P(DP, MP),) * 7, P())
    return jax.shard_map(
        local,
        mesh=split,
        in_specs=placed,
        out_specs=(P(DP, MP), P(DP, MP), P(DP, MP), P(MP, DP)),
        check_vma=False,
    )
```
